32 devices in a mesh: pair: 32 (over z, y, x, core), red: 1.
Axes of the slice: x: 2, y: 2, z: 4, core: 2. Of those that a mesh axis runs over, the one named last changes fastest.
Arguments:
- integrals: bfloat16 [256, 64, 1536], P(('pair', 'red')), may hold values from -6 to 6
- coeffs: bfloat16 [6016, 256], replicated, may hold values from -0.078125 to 0.078125
- shell_pairs: int32 [256, 2], replicated, may hold values from 0 to 93, as said below
- block_count: int32 [32, 1], P('pair', 'red'), may hold values from 1 to 8, as said below
Outputs:
- mo_ints: float32 [256, 24, 256], P('pair', None, 'red')
The draws below stay inside these ranges and needn't reach their ends.
Inputs may be any that keep to these rules, and one draw needn't show every extreme that they name: `shell_pairs`: the 256 rows are distinct shell pairs (row shell, column shell). `block_count`: some device has all 8 slots live.
All inputs are finite; a program needn't handle non-finite values.
Results may differ from the reference program's by a relative error of at most 0.0029.
Values may be sent and summed in bfloat16 or wider, within the bound.
A program may use at most 128 MiB of HBM per device.

```python
import jax
import jax.numpy as jnp
from jax import lax

SHELL_WIDTH = 64
SHELL_BLOCKS = 94
NAO = 6016
OCCUPIED_COUNT = 256
KET_PAIRS = 24
BLK_CAP = 8
TOTAL_SLOTS = 256
N_PAIR = 32
N_RED = 1


def draw_shell_pairs(key, part):
    key = jax.random.fold_in(key, 11)
    selected_blocks = jax.random.permutation(key, SHELL_BLOCKS * SHELL_BLOCKS)[:TOTAL_SLOTS]
    return jnp.stack([selected_blocks // SHELL_BLOCKS, selected_blocks % SHELL_BLOCKS], axis=1).astype(jnp.int32)


def draw_block_count(key, part):
    key = jax.random.fold_in(key, 23)
    first_key, second_key = jax.random.split(key)
    counts = jax.random.randint(first_key, (N_PAIR * N_RED,), 1, BLK_CAP + 1)
    fullest = jax.random.randint(second_key, (), 0, N_PAIR * N_RED)
    counts = jnp.where(jnp.arange(N_PAIR * N_RED) == fullest, BLK_CAP, counts)
    return counts.reshape(N_PAIR, N_RED).astype(jnp.int32)


def shard_levels(stream_key, dims, cuts, least, top_value):
    factor_of, own = 1.0, jax.random.fold_in(stream_key, 6)
    for axis_at, shards_of in cuts:
        steps = jnp.exp(jax.random.uniform(jax.random.fold_in(own, axis_at), (shards_of,), jnp.float32, least / len(cuts), top_value / len(cuts)))
        factor_of = factor_of * jnp.repeat(steps, dims[axis_at] // shards_of).reshape([-1 if axis == axis_at else 1 for axis in range(len(dims))])
    return factor_of


def bell_draw(key, extent, spread, most, shards=(), held_as=jnp.bfloat16):
    level = shard_levels(key, extent, shards, -0.22, 0.18) if shards else 1.0
    result = jax.random.normal(key, extent, jnp.float32) * spread * level
    return jnp.minimum(jnp.maximum(result, -most), most).astype(held_as)


def setup_inputs(seed: int = 0) -> dict:
    keys = jax.random.split(jax.random.key(seed), 5)
    return {
        "integrals": bell_draw(keys[0], (TOTAL_SLOTS, SHELL_WIDTH, KET_PAIRS * SHELL_WIDTH), 1.0, 6.0, ((0, 32),)),
        "coeffs": bell_draw(keys[1], (NAO, OCCUPIED_COUNT), NAO ** -0.5, 0.078125),
        "shell_pairs": draw_shell_pairs(jax.random.fold_in(keys[4], 71), 0),
        "block_count": draw_block_count(jax.random.fold_in(keys[4], 71), 0),
    }


def reference(integrals, coeffs, shell_pairs, block_count):
    live_counts = block_count.reshape(-1)
    coef_table = coeffs.reshape(SHELL_BLOCKS, SHELL_WIDTH, OCCUPIED_COUNT).astype(jnp.float32)

    def block_adder(collected_blocks, slot_index):
        row_shell = shell_pairs[slot_index, 0]
        col_shell = shell_pairs[slot_index, 1]
        live_mask = ((slot_index % BLK_CAP) < live_counts[slot_index // BLK_CAP]).astype(jnp.float32)
        left_panel = lax.dynamic_index_in_dim(coef_table, row_shell, 0, keepdims=False)
        tile_block = lax.dynamic_index_in_dim(integrals, slot_index, 0, keepdims=False).astype(jnp.float32)
        half_done = jnp.dot(left_panel.T, tile_block, precision=lax.Precision.HIGHEST) * live_mask
        half_done = lax.optimization_barrier(half_done.astype(jnp.bfloat16))
        half_done = half_done.astype(jnp.float32).reshape(OCCUPIED_COUNT * KET_PAIRS, SHELL_WIDTH)
        current = lax.dynamic_index_in_dim(collected_blocks, col_shell, 0, keepdims=False)
        collected_blocks = lax.dynamic_update_index_in_dim(collected_blocks, current + half_done, col_shell, 0)
        return collected_blocks, None

    collected_blocks, unused_value = lax.scan(block_adder, jnp.zeros((SHELL_BLOCKS, OCCUPIED_COUNT * KET_PAIRS, SHELL_WIDTH), jnp.float32), jnp.arange(TOTAL_SLOTS, dtype=jnp.int32))
    mo_flat = jnp.einsum("tan,tnj->aj", collected_blocks, coef_table, precision=lax.Precision.HIGHEST)
    return mo_flat.reshape(OCCUPIED_COUNT, KET_PAIRS, OCCUPIED_COUNT)
```

```python
import functools
import math

import jax
import jax.numpy as jnp
from jax import lax
from jax.experimental import pallas as pl
from jax.experimental.pallas import tpu as pltpu
from jax.sharding import PartitionSpec as P

GROUPS = 6
LOW_EXP = -80.0


def encode(x, steps):
    level = jnp.log(jnp.abs(x)) * (steps / math.log(2.0)) + (0.5 - LOW_EXP * steps)
    code = jnp.clip(level, 0.0, 32767.0).astype(jnp.int32)
    return jnp.where(x < 0.0, -code, code).astype(jnp.int16)


def decode(code, steps):
    wide = code.astype(jnp.int32).astype(jnp.float32)
    size = jnp.exp2(jnp.abs(wide) * (1.0 / steps) + LOW_EXP)
    value = jnp.where(wide < 0.0, -size, size)
    return jnp.where(wide == 0.0, 0.0, value)


def transform_kernel(
    steps,
    pairs_ref, count_ref, coeffs_hbm, ints_hbm, out_ref,
    coeffs, ints, turned, left, right, diag,
    own, snd0, rcv0, snd1, rcv1, snd2, rcv2, snd3, rcv3,
    load_sem, send_sem, recv_sem,
):
    load_coeffs = pltpu.make_async_copy(coeffs_hbm, coeffs, load_sem.at[0])
    load_ints = pltpu.make_async_copy(ints_hbm, ints, load_sem.at[1])
    load_coeffs.start()
    load_ints.start()

    me = lax.axis_index("pair")

    def other(bit):
        return me + bit * (1 - 2 * ((me // bit) % 2))

    core_at, x_at, y_at = other(1), other(2), other(4)
    z_low, z_high = other(8) - me, other(16) - me
    z_at = (me + z_low, me + z_high, me + z_low + z_high)
    partners = (core_at, x_at, y_at) + z_at

    barrier = pltpu.get_barrier_semaphore()
    for at in partners:
        pl.semaphore_signal(
            barrier, inc=1, device_id={"pair": at}, device_id_type=pl.DeviceIdType.MESH
        )

    slots, width, columns = ints.shape
    occ = coeffs.shape[2]
    span = 4 * width
    diag[...] = jnp.zeros_like(diag)
    load_coeffs.wait()
    for k in range(slots):
        row_shell = pairs_ref[me * slots + k, 0]
        col_shell = pairs_ref[me * slots + k, 1]
        live = jnp.where(k < count_ref[0, 0], 1.0, 0.0).astype(jnp.float32)
        panel = coeffs[row_shell].astype(jnp.float32) * live
        turned[k // 4, :, :, pl.ds((k % 4) * width, width)] = panel.T.reshape(
            occ // 8, 8, width
        )
        right[pl.ds(k * width, width), :] = coeffs[col_shell]

    bits = [(me // w) % 2 for w in (1, 2, 4, 8, 16)]

    def place(rel):
        return sum(((rel // w) % 2 + b - 2 * ((rel // w) % 2) * b) * w
                   for w, b in zip((1, 2, 4, 8, 16), bits))

    for core in range(2):
        for two in range(8):
            first = place(core + 2 * (2 * two))
            second = place(core + 2 * (2 * two + 1))
            for part in range(2):
                rows = jnp.concatenate([turned[part, first], turned[part, second]], axis=0)
                left[part, pl.ds(core * 128 + two * 16, 16), :] = rows.astype(jnp.bfloat16)

    load_ints.wait()

    lane = lax.broadcasted_iota(jnp.int32, (width, 2 * width), 1)
    low = lane < width
    per_group = columns // (2 * width) // GROUPS

    def compute(group):
        def one_pair(step, carry):
            cols = pl.ds(pl.multiple_of((group * per_group + step) * 2 * width, 2 * width), 2 * width)
            for k in range(slots):
                tile = ints[k, :, cols].astype(jnp.float32)
                swap = pltpu.roll(tile, width, 1)
                at_lane = pl.ds((k % 4) // 2 * 2 * width, 2 * width)
                at_row = pl.ds((k % 4) * width, width)
                for odd in range(2):
                    source = tile if k % 2 == odd else swap
                    keep = low if k % 2 == 0 else jnp.logical_not(low)
                    diag[odd, k // 4, at_row, at_lane] = jnp.where(keep, source, 0.0).astype(jnp.bfloat16)
            done = []
            for odd in range(2):
                half = jnp.concatenate(
                    [
                        jnp.dot(left[part], diag[odd, part], preferred_element_type=jnp.float32).astype(jnp.bfloat16)
                        for part in range(2)
                    ],
                    axis=1,
                )
                done.append(jnp.dot(half, right[...], preferred_element_type=jnp.float32).reshape(2, 4, 2, 2, 8, occ))
            both = jnp.concatenate(done, axis=4)
            own[group, :, :, :, step] = both[0]
            snd0[group, :, :, :, step] = both[1].astype(jnp.bfloat16)
            return carry

        lax.fori_loop(0, per_group, one_pair, 0)

    def copy(group, stage, source, target, at):
        return pltpu.make_async_remote_copy(
            src_ref=source,
            dst_ref=target,
            send_sem=send_sem.at[group, stage],
            recv_sem=recv_sem.at[group, stage],
            device_id={"pair": at},
            device_id_type=pl.DeviceIdType.MESH,
        )

    def copies(group):
        first, second = (x_at, y_at) if group % 2 == 0 else (y_at, x_at)
        made = [
            copy(group, 0, snd0.at[group], rcv0.at[group], core_at),
            copy(group, 1, snd1.at[group], rcv1.at[group], first),
            copy(group, 2, snd2.at[group], rcv2.at[group], second),
        ]
        for n in range(3):
            made.append(copy(group, 3 + n, snd3.at[group, n], rcv3.at[group, n], z_at[n]))
        return made

    plan = [copies(group) for group in range(GROUPS)]

    def chunk(group, z, a, b):
        y, x = (a, b) if group % 2 == 0 else (b, a)
        return own[group, z, y, x] + rcv0[group, z, y, x].astype(jnp.float32)

    def stage1(group):
        plan[group][0].wait_recv()

        def body(z, carry):
            for a in range(2):
                snd1[group, z, a] = encode(chunk(group, z, a, 1), steps)
            return carry

        lax.fori_loop(0, 4, body, 0)
        plan[group][1].start()

    def stage2(group):
        plan[group][1].wait_recv()

        def body(z, carry):
            total = chunk(group, z, 1, 0) + decode(rcv1[group, z, 1], steps)
            snd2[group, z] = encode(total, steps)
            return carry

        lax.fori_loop(0, 4, body, 0)
        plan[group][2].start()

    def gathered(group, z):
        return (
            chunk(group, z, 0, 0)
            + decode(rcv1[group, z, 0], steps)
            + decode(rcv2[group, z], steps)
        )

    def stage3(group):
        plan[group][2].wait_recv()
        for n in (1, 2, 0):
            snd3[group, n] = encode(gathered(group, n + 1), steps)
            plan[group][3 + n].start()

    def finish(group):
        total = gathered(group, 0)
        for n in range(3):
            plan[group][3 + n].wait_recv()
            total = total + decode(rcv3[group, n], steps)
        out_ref[group] = total

    stages = (stage1, stage2, stage3, finish)
    for tick in range(GROUPS + len(stages)):
        if tick < GROUPS:
            compute(tick)
            if tick == 0:
                pl.semaphore_wait(barrier, len(partners))
            plan[tick][0].start()
        for later, stage in enumerate(stages):
            if 0 <= tick - 1 - later < GROUPS:
                stage(tick - 1 - later)
    for group in range(GROUPS):
        for item in plan[group]:
            item.wait_send()


def on_device(integrals, coeffs, shell_pairs, block_count):
    slots, width, columns = integrals.shape
    occ = coeffs.shape[1]
    kets = columns // width
    shells = coeffs.shape[0] // width
    per_group = kets // 2 // GROUPS
    top = math.ceil(math.log2(shell_pairs.shape[0] * width * width * 6 * 0.078125 ** 2)) + 1
    steps = 32760.0 / (top - LOW_EXP)
    tile = (per_group, 16, occ)
    bf16, i16 = jnp.bfloat16, jnp.int16
    hbm = pl.BlockSpec(memory_space=pl.ANY)
    smem = pl.BlockSpec(memory_space=pltpu.SMEM)
    out = pl.pallas_call(
        functools.partial(transform_kernel, steps),
        out_shape=jax.ShapeDtypeStruct((GROUPS,) + tile, jnp.float32),
        in_specs=[smem, smem, hbm, hbm],
        out_specs=pl.BlockSpec(memory_space=pltpu.VMEM),
        scratch_shapes=[
            pltpu.VMEM((shells, width, occ), bf16),
            pltpu.VMEM(integrals.shape, bf16),
            pltpu.VMEM((2, occ // 8, 8, 4 * width), jnp.float32),
            pltpu.VMEM((2, occ, 4 * width), bf16),
            pltpu.VMEM((slots * width, occ), bf16),
            pltpu.VMEM((2, 2, 4 * width, 4 * width), bf16),
            pltpu.VMEM((GROUPS, 4, 2, 2) + tile, jnp.float32),
            pltpu.VMEM((GROUPS, 4, 2, 2) + tile, bf16),
            pltpu.VMEM((GROUPS, 4, 2, 2) + tile, bf16),
            pltpu.VMEM((GROUPS, 4, 2) + tile, i16),
            pltpu.VMEM((GROUPS, 4, 2) + tile, i16),
            pltpu.VMEM((GROUPS, 4) + tile, i16),
            pltpu.VMEM((GROUPS, 4) + tile, i16),
            pltpu.VMEM((GROUPS, 3) + tile, i16),
            pltpu.VMEM((GROUPS, 3) + tile, i16),
            pltpu.SemaphoreType.DMA((2,)),
            pltpu.SemaphoreType.DMA((GROUPS, 6)),
            pltpu.SemaphoreType.DMA((GROUPS, 6)),
        ],
        compiler_params=pltpu.CompilerParams(
            collective_id=0, has_side_effects=True, vmem_limit_bytes=48 * 1024 * 1024
        ),
    )(shell_pairs, block_count, coeffs.reshape(shells, width, occ), integrals)
    return out.reshape(kets, occ // 32, occ).transpose(1, 0, 2)


def on_device_general(integrals, coeffs, shell_pairs, block_count):
    slot_count = integrals.shape[0]
    shell_size = integrals.shape[1]
    ket_count = integrals.shape[2] // shell_size
    occ_count = coeffs.shape[1]
    shell_count = coeffs.shape[0] // shell_size
    pair_count = lax.axis_size("pair")
    red_count = lax.axis_size("red")
    pair_index = lax.axis_index("pair")
    red_index = lax.axis_index("red")
    owned_rows = occ_count // pair_count
    coef_table = coeffs.reshape(shell_count, shell_size, occ_count)
    first_slot = (pair_index * red_count + red_index) * slot_count
    own_pairs = lax.dynamic_slice_in_dim(shell_pairs, first_slot, slot_count, 0)
    live_mask = (jnp.arange(slot_count, dtype=jnp.int32) < block_count[0, 0]).astype(jnp.float32)
    left_panels = jnp.take(coef_table, own_pairs[:, 0], axis=0)
    half_done = jnp.einsum(
        "kmi,kmx->kix", left_panels, integrals, preferred_element_type=jnp.float32
    )
    half_done = (half_done * live_mask[:, None, None]).astype(jnp.bfloat16)
    right_panels = jnp.take(coef_table, own_pairs[:, 1], axis=0)
    whole_sum = jnp.einsum(
        "kpiqn,knrj->priqj",
        half_done.reshape(slot_count, pair_count, owned_rows, ket_count, shell_size),
        right_panels.reshape(slot_count, shell_size, red_count, occ_count // red_count),
        preferred_element_type=jnp.float32,
    )
    whole_sum = whole_sum.reshape(
        pair_count * red_count * owned_rows, ket_count, occ_count // red_count
    )
    return lax.psum_scatter(whole_sum, ("pair", "red"), scatter_dimension=0, tiled=True)


def solution(mesh):
    small = mesh.shape["pair"] == 32 and mesh.shape["red"] == 1
    return jax.shard_map(
        on_device if small else on_device_general,
        mesh=mesh,
        in_specs=(P(("pair", "red"), None, None), P(), P(), P("pair", "red")),
        out_specs=P("pair", None, "red"),
        check_vma=False,
    )
```

```python
import functools
import math

import jax
import jax.numpy as jnp
from jax import lax
from jax.experimental import pallas as pl
from jax.experimental.pallas import tpu as pltpu
from jax.sharding import PartitionSpec as P

GROUPS = 12
LAGS = (1, 3, 5, 7)
LOW_EXP = -80.0


def encode(x, steps):
    level = jnp.log(jnp.abs(x)) * (steps / math.log(2.0)) + (0.5 - LOW_EXP * steps)
    level = jnp.maximum(level, 0.0)
    return jnp.where(x < 0.0, -level, level).astype(jnp.int32).astype(jnp.int16)


def decode(code, steps):
    wide = code.astype(jnp.int32).astype(jnp.float32)
    size = jnp.exp2(jnp.abs(wide) * (1.0 / steps) + LOW_EXP)
    value = jnp.where(wide < 0.0, -size, size)
    return jnp.where(wide == 0.0, 0.0, value)


def transform_kernel(
    steps,
    pairs_ref, count_ref, coeffs_hbm, ints_hbm, out_ref,
    coeffs, ints, turned, left, right, diag,
    own, snd0, rcv0, snd1, rcv1, snd2, rcv2, snd3, rcv3,
    load_sem, send_sem, recv_sem,
):
    load_coeffs = pltpu.make_async_copy(coeffs_hbm, coeffs, load_sem.at[0])
    load_ints = pltpu.make_async_copy(ints_hbm, ints, load_sem.at[1])
    load_coeffs.start()
    load_ints.start()

    me = lax.axis_index("pair")

    def other(bit):
        return me + bit * (1 - 2 * ((me // bit) % 2))

    core_at, x_at, y_at = other(1), other(2), other(4)
    z_low, z_high = other(8) - me, other(16) - me
    z_at = (me + z_low, me + z_high, me + z_low + z_high)
    partners = (core_at, x_at, y_at) + z_at

    barrier = pltpu.get_barrier_semaphore()
    for at in partners:
        pl.semaphore_signal(
            barrier, inc=1, device_id={"pair": at}, device_id_type=pl.DeviceIdType.MESH
        )

    slots, width, columns = ints.shape
    occ = coeffs.shape[2]
    span = 4 * width
    diag[...] = jnp.zeros_like(diag)
    load_coeffs.wait()
    for k in range(slots):
        row_shell = pairs_ref[0, me * slots + k]
        col_shell = pairs_ref[1, me * slots + k]
        live = jnp.where(k < count_ref[0, 0], 1.0, 0.0).astype(jnp.float32)
        panel = coeffs[row_shell].astype(jnp.float32) * live
        turned[k // 4, :, :, pl.ds((k % 4) * width, width)] = panel.T.reshape(
            occ // 8, 8, width
        )
        right[pl.ds(k * width, width), :] = coeffs[col_shell]

    bits = [(me // w) % 2 for w in (1, 2, 4, 8, 16)]

    def place(rel):
        return sum(((rel // w) % 2 + b - 2 * ((rel // w) % 2) * b) * w
                   for w, b in zip((1, 2, 4, 8, 16), bits))

    for core in range(2):
        for two in range(8):
            first = place(core + 2 * (2 * two))
            second = place(core + 2 * (2 * two + 1))
            for part in range(2):
                rows = jnp.concatenate([turned[part, first], turned[part, second]], axis=0)
                left[part, pl.ds(core * 128 + two * 16, 16), :] = rows.astype(jnp.bfloat16)

    load_ints.wait()

    lane = lax.broadcasted_iota(jnp.int32, (width, 2 * width), 1)
    low = lane < width
    per_group = columns // (2 * width) // GROUPS

    def compute(group):
        def one_pair(step, carry):
            cols = pl.ds(pl.multiple_of((group * per_group + step) * 2 * width, 2 * width), 2 * width)
            for k in range(slots):
                tile = ints[k, :, cols].astype(jnp.float32)
                swap = pltpu.roll(tile, width, 1)
                at_lane = pl.ds((k % 4) // 2 * 2 * width, 2 * width)
                at_row = pl.ds((k % 4) * width, width)
                for odd in range(2):
                    source = tile if k % 2 == odd else swap
                    keep = low if k % 2 == 0 else jnp.logical_not(low)
                    diag[odd, k // 4, at_row, at_lane] = jnp.where(keep, source, 0.0).astype(jnp.bfloat16)
            done = []
            for odd in range(2):
                half = jnp.concatenate(
                    [
                        jnp.dot(left[part], diag[odd, part], preferred_element_type=jnp.float32).astype(jnp.bfloat16)
                        for part in range(2)
                    ],
                    axis=1,
                )
                done.append(jnp.dot(half, right[...], preferred_element_type=jnp.float32).reshape(2, 4, 2, 2, 8, occ))
            both = jnp.concatenate(done, axis=4)
            own[group, :, :, :, step] = both[0]
            snd0[group, :, :, :, step] = both[1].astype(jnp.bfloat16)
            return carry

        lax.fori_loop(0, per_group, one_pair, 0)

    def copy(group, stage, source, target, at):
        return pltpu.make_async_remote_copy(
            src_ref=source,
            dst_ref=target,
            send_sem=send_sem.at[group, stage],
            recv_sem=recv_sem.at[group, stage],
            device_id={"pair": at},
            device_id_type=pl.DeviceIdType.MESH,
        )

    def core_copy(group):
        return copy(group, 0, snd0.at[group], rcv0.at[group], core_at)

    def first_copy(group, kind):
        at = y_at if kind else x_at
        return copy(group, 1, snd1.at[group], rcv1.at[group], at)

    def second_copy(group, kind):
        at = x_at if kind else y_at
        return copy(group, 2, snd2.at[group], rcv2.at[group], at)

    def z_copy(group, n):
        return copy(group, 3 + n, snd3.at[group, n], rcv3.at[group, n], z_at[n])

    def chunks(group, kind, z, a, b):
        y, x = (a, b) if kind == 0 else (b, a)
        return own[group, z, y, x] + rcv0[group, z, y, x].astype(jnp.float32)

    def stage1(group, kind):
        core_copy(group).wait_recv()
        snd1[group] = encode(chunks(group, kind, slice(None), slice(None), 1), steps)
        first_copy(group, kind).start()

    def stage2(group, kind):
        first_copy(group, kind).wait_recv()
        total = chunks(group, kind, slice(None), 1, 0) + decode(rcv1[group, :, 1], steps)
        snd2[group] = encode(total, steps)
        second_copy(group, kind).start()

    def gathered(group, kind, z):
        return (
            chunks(group, kind, z, 0, 0)
            + decode(rcv1[group, z, 0], steps)
            + decode(rcv2[group, z], steps)
        )

    def stage3(group, kind):
        second_copy(group, kind).wait_recv()
        for n in (1, 2, 0):
            snd3[group, n] = encode(gathered(group, kind, n + 1), steps)
            z_copy(group, n).start()

    def finish(group, kind):
        total = gathered(group, kind, 0)
        for n in range(3):
            z_copy(group, n).wait_recv()
        total = total + jnp.sum(decode(rcv3[group], steps), axis=0)
        out_ref[group] = total

    stages = (stage1, stage2, stage3, finish)

    def two_ticks(turn, carry):
        for kind in range(2):
            tick = 2 * turn + kind

            @pl.when(tick < GROUPS)
            def _():
                compute(tick)
                if kind == 0:
                    @pl.when(turn == 0)
                    def _():
                        pl.semaphore_wait(barrier, len(partners))
                core_copy(tick).start()

            for lag, stage in zip(LAGS, stages):
                group = tick - lag

                @pl.when(jnp.logical_and(group >= 0, group < GROUPS))
                def _(group=group, stage=stage):
                    stage(group, 1 - kind)
        return carry

    lax.fori_loop(0, (GROUPS + LAGS[-1] + 1) // 2, two_ticks, 0)

    def drain(half, carry):
        for kind in range(2):
            group = 2 * half + kind
            core_copy(group).wait_send()
            first_copy(group, kind).wait_send()
            second_copy(group, kind).wait_send()
            for n in range(3):
                z_copy(group, n).wait_send()
        return carry

    lax.fori_loop(0, GROUPS // 2, drain, 0)


def on_device(integrals, coeffs, shell_pairs, block_count):
    slots, width, columns = integrals.shape
    occ = coeffs.shape[1]
    kets = columns // width
    shells = coeffs.shape[0] // width
    per_group = kets // 2 // GROUPS
    top = math.ceil(math.log2(shell_pairs.shape[0] * width * width * 6 * 0.078125 ** 2)) + 1
    steps = 32760.0 / (top - LOW_EXP)
    tile = (per_group, 16, occ)
    bf16, i16 = jnp.bfloat16, jnp.int16
    hbm = pl.BlockSpec(memory_space=pl.ANY)
    smem = pl.BlockSpec(memory_space=pltpu.SMEM)
    out = pl.pallas_call(
        functools.partial(transform_kernel, steps),
        out_shape=jax.ShapeDtypeStruct((GROUPS,) + tile, jnp.float32),
        in_specs=[smem, smem, hbm, hbm],
        out_specs=pl.BlockSpec(memory_space=pltpu.VMEM),
        scratch_shapes=[
            pltpu.VMEM((shells, width, occ), bf16),
            pltpu.VMEM(integrals.shape, bf16),
            pltpu.VMEM((2, occ // 8, 8, 4 * width), jnp.float32),
            pltpu.VMEM((2, occ, 4 * width), bf16),
            pltpu.VMEM((slots * width, occ), bf16),
            pltpu.VMEM((2, 2, 4 * width, 4 * width), bf16),
            pltpu.VMEM((GROUPS, 4, 2, 2) + tile, jnp.float32),
            pltpu.VMEM((GROUPS, 4, 2, 2) + tile, bf16),
            pltpu.VMEM((GROUPS, 4, 2, 2) + tile, bf16),
            pltpu.VMEM((GROUPS, 4, 2) + tile, i16),
            pltpu.VMEM((GROUPS, 4, 2) + tile, i16),
            pltpu.VMEM((GROUPS, 4) + tile, i16),
            pltpu.VMEM((GROUPS, 4) + tile, i16),
            pltpu.VMEM((GROUPS, 3) + tile, i16),
            pltpu.VMEM((GROUPS, 3) + tile, i16),
            pltpu.SemaphoreType.DMA((2,)),
            pltpu.SemaphoreType.DMA((GROUPS, 6)),
            pltpu.SemaphoreType.DMA((GROUPS, 6)),
        ],
        compiler_params=pltpu.CompilerParams(
            collective_id=0, has_side_effects=True, vmem_limit_bytes=60 * 1024 * 1024
        ),
    )(shell_pairs.T, block_count, coeffs.reshape(shells, width, occ), integrals)
    return out.reshape(kets, occ // 32, occ).transpose(1, 0, 2)


def on_device_general(integrals, coeffs, shell_pairs, block_count):
    slot_count = integrals.shape[0]
    shell_size = integrals.shape[1]
    ket_count = integrals.shape[2] // shell_size
    occ_count = coeffs.shape[1]
    shell_count = coeffs.shape[0] // shell_size
    pair_count = lax.axis_size("pair")
    red_count = lax.axis_size("red")
    pair_index = lax.axis_index("pair")
    red_index = lax.axis_index("red")
    owned_rows = occ_count // pair_count
    coef_table = coeffs.reshape(shell_count, shell_size, occ_count)
    first_slot = (pair_index * red_count + red_index) * slot_count
    own_pairs = lax.dynamic_slice_in_dim(shell_pairs, first_slot, slot_count, 0)
    live_mask = (jnp.arange(slot_count, dtype=jnp.int32) < block_count[0, 0]).astype(jnp.float32)
    left_panels = jnp.take(coef_table, own_pairs[:, 0], axis=0)
    half_done = jnp.einsum(
        "kmi,kmx->kix", left_panels, integrals, preferred_element_type=jnp.float32
    )
    half_done = (half_done * live_mask[:, None, None]).astype(jnp.bfloat16)
    right_panels = jnp.take(coef_table, own_pairs[:, 1], axis=0)
    whole_sum = jnp.einsum(
        "kpiqn,knrj->priqj",
        half_done.reshape(slot_count, pair_count, owned_rows, ket_count, shell_size),
        right_panels.reshape(slot_count, shell_size, red_count, occ_count // red_count),
        preferred_element_type=jnp.float32,
    )
    whole_sum = whole_sum.reshape(
        pair_count * red_count * owned_rows, ket_count, occ_count // red_count
    )
    return lax.psum_scatter(whole_sum, ("pair", "red"), scatter_dimension=0, tiled=True)


def solution(mesh):
    small = mesh.shape["pair"] == 32 and mesh.shape["red"] == 1
    return jax.shard_map(
        on_device if small else on_device_general,
        mesh=mesh,
        in_specs=(P(("pair", "red"), None, None), P(), P(), P("pair", "red")),
        out_specs=P("pair", None, "red"),
        check_vma=False,
    )
```

```python
import functools
import math

import jax
import jax.numpy as jnp
from jax import lax
from jax.experimental import pallas as pl
from jax.experimental.pallas import tpu as pltpu
from jax.sharding import PartitionSpec as P

GROUPS = 12
LAGS = (1, 5, 9, 13)
LOW_EXP = -80.0


def encode(x, steps):
    level = jnp.log(jnp.abs(x)) * (steps / math.log(2.0)) + (0.5 - LOW_EXP * steps)
    level = jnp.maximum(level, 0.0)
    return jnp.where(x < 0.0, -level, level).astype(jnp.int32).astype(jnp.int16)


def decode(code, steps):
    wide = code.astype(jnp.int32).astype(jnp.float32)
    size = jnp.exp2(jnp.abs(wide) * (1.0 / steps) + LOW_EXP)
    value = jnp.where(wide < 0.0, -size, size)
    return jnp.where(wide == 0.0, 0.0, value)


def transform_kernel(
    steps,
    pairs_ref, count_ref, coeffs_hbm, ints_hbm, out_ref,
    coeffs, ints, turned, left, right, diag,
    own, snd0, rcv0, snd1, rcv1, snd2, rcv2, snd3, rcv3,
    load_sem, send_sem, recv_sem,
):
    load_coeffs = pltpu.make_async_copy(coeffs_hbm, coeffs, load_sem.at[0])
    load_ints = pltpu.make_async_copy(ints_hbm, ints, load_sem.at[1])
    load_coeffs.start()
    load_ints.start()

    me = lax.axis_index("pair")

    def other(bit):
        return me + bit * (1 - 2 * ((me // bit) % 2))

    core_at, x_at, y_at = other(1), other(2), other(4)
    z_low, z_high = other(8) - me, other(16) - me
    z_at = (me + z_low, me + z_high, me + z_low + z_high)
    partners = (core_at, x_at, y_at) + z_at

    barrier = pltpu.get_barrier_semaphore()
    for at in partners:
        pl.semaphore_signal(
            barrier, inc=1, device_id={"pair": at}, device_id_type=pl.DeviceIdType.MESH
        )

    slots, width, columns = ints.shape
    occ = coeffs.shape[2]
    span = 4 * width
    diag[...] = jnp.zeros_like(diag)
    load_coeffs.wait()
    for k in range(slots):
        row_shell = pairs_ref[0, me * slots + k]
        col_shell = pairs_ref[1, me * slots + k]
        live = jnp.where(k < count_ref[0, 0], 1.0, 0.0).astype(jnp.float32)
        panel = coeffs[row_shell].astype(jnp.float32) * live
        turned[k // 4, :, :, pl.ds((k % 4) * width, width)] = panel.T.reshape(
            occ // 8, 8, width
        )
        right[pl.ds(k * width, width), :] = coeffs[col_shell]

    moves = [other(w) - me for w in (1, 2, 4, 8, 16)]

    def place(rel):
        at = me
        for n, move in enumerate(moves):
            if (rel >> n) % 2:
                at = at + move
        return at

    for core in range(2):
        for two in range(8):
            first = place(core + 2 * (2 * two))
            second = place(core + 2 * (2 * two + 1))
            for part in range(2):
                rows = jnp.concatenate([turned[part, first], turned[part, second]], axis=0)
                left[part, pl.ds(core * 128 + two * 16, 16), :] = rows.astype(jnp.bfloat16)

    load_ints.wait()

    lane = lax.broadcasted_iota(jnp.int32, (width, 2 * width), 1)
    low = lane < width
    per_group = columns // (2 * width) // GROUPS

    def compute(group):
        def one_pair(step, carry):
            cols = pl.ds(pl.multiple_of((group * per_group + step) * 2 * width, 2 * width), 2 * width)
            for k in range(slots):
                tile = ints[k, :, cols].astype(jnp.float32)
                swap = pltpu.roll(tile, width, 1)
                at_lane = pl.ds((k % 4) // 2 * 2 * width, 2 * width)
                at_row = pl.ds((k % 4) * width, width)
                for odd in range(2):
                    source = tile if k % 2 == odd else swap
                    keep = low if k % 2 == 0 else jnp.logical_not(low)
                    diag[odd, k // 4, at_row, at_lane] = jnp.where(keep, source, 0.0).astype(jnp.bfloat16)
            done = []
            for odd in range(2):
                half = jnp.concatenate(
                    [
                        jnp.dot(left[part], diag[odd, part], preferred_element_type=jnp.float32).astype(jnp.bfloat16)
                        for part in range(2)
                    ],
                    axis=1,
                )
                done.append(jnp.dot(half, right[...], preferred_element_type=jnp.float32).reshape(2, 4, 2, 2, 8, occ))
            both = jnp.concatenate(done, axis=4)
            own[group, :, :, :, step] = both[0]
            snd0[group, :, :, :, step] = both[1].astype(jnp.bfloat16)
            return carry

        lax.fori_loop(0, per_group, one_pair, 0)

    def copy(group, stage, source, target, at):
        return pltpu.make_async_remote_copy(
            src_ref=source,
            dst_ref=target,
            send_sem=send_sem.at[group, stage],
            recv_sem=recv_sem.at[group, stage],
            device_id={"pair": at},
            device_id_type=pl.DeviceIdType.MESH,
        )

    def core_copy(group):
        return copy(group, 0, snd0.at[group], rcv0.at[group], core_at)

    def first_copy(group, kind):
        at = y_at if kind else x_at
        return copy(group, 1, snd1.at[group], rcv1.at[group], at)

    def second_copy(group, kind):
        at = x_at if kind else y_at
        return copy(group, 2, snd2.at[group], rcv2.at[group], at)

    def z_copy(group, n):
        return copy(group, 3 + n, snd3.at[group, n], rcv3.at[group, n], z_at[n])

    def chunks(group, kind, z, a, b):
        y, x = (a, b) if kind == 0 else (b, a)
        return own[group, z, y, x] + rcv0[group, z, y, x].astype(jnp.float32)

    def stage1(group, kind):
        core_copy(group).wait_recv()
        snd1[group] = chunks(group, kind, slice(None), slice(None), 1).astype(jnp.bfloat16)
        first_copy(group, kind).start()

    def stage2(group, kind):
        first_copy(group, kind).wait_recv()
        total = chunks(group, kind, slice(None), 1, 0) + rcv1[group, :, 1].astype(jnp.float32)
        snd2[group] = encode(total, steps)
        second_copy(group, kind).start()

    def gathered(group, kind, z):
        return (
            chunks(group, kind, z, 0, 0)
            + rcv1[group, z, 0].astype(jnp.float32)
            + decode(rcv2[group, z], steps)
        )

    def stage3(group, kind):
        second_copy(group, kind).wait_recv()
        for n in (1, 2, 0):
            snd3[group, n] = encode(gathered(group, kind, n + 1), steps)
            z_copy(group, n).start()

    def finish(group, kind):
        total = gathered(group, kind, 0)
        for n in range(3):
            z_copy(group, n).wait_recv()
        total = total + jnp.sum(decode(rcv3[group], steps), axis=0)
        out_ref[group] = total

    stages = (stage1, stage2, stage3, finish)

    def two_ticks(turn, carry):
        for kind in range(2):
            tick = 2 * turn + kind

            @pl.when(tick < GROUPS)
            def _():
                compute(tick)
                if kind == 0:
                    @pl.when(turn == 0)
                    def _():
                        pl.semaphore_wait(barrier, len(partners))
                core_copy(tick).start()

            for lag, stage in zip(LAGS, stages):
                group = tick - lag

                @pl.when(jnp.logical_and(group >= 0, group < GROUPS))
                def _(group=group, stage=stage):
                    stage(group, 1 - kind)
        return carry

    lax.fori_loop(0, (GROUPS + LAGS[-1] + 1) // 2, two_ticks, 0)

    def drain(half, carry):
        for kind in range(2):
            group = 2 * half + kind
            core_copy(group).wait_send()
            first_copy(group, kind).wait_send()
            second_copy(group, kind).wait_send()
            for n in range(3):
                z_copy(group, n).wait_send()
        return carry

    lax.fori_loop(0, GROUPS // 2, drain, 0)


def on_device(integrals, coeffs, shell_pairs, block_count):
    slots, width, columns = integrals.shape
    occ = coeffs.shape[1]
    kets = columns // width
    shells = coeffs.shape[0] // width
    per_group = kets // 2 // GROUPS
    top = math.ceil(math.log2(shell_pairs.shape[0] * width * width * 6 * 0.078125 ** 2)) + 1
    steps = 32760.0 / (top - LOW_EXP)
    tile = (per_group, 16, occ)
    bf16, i16 = jnp.bfloat16, jnp.int16
    hbm = pl.BlockSpec(memory_space=pl.ANY)
    smem = pl.BlockSpec(memory_space=pltpu.SMEM)
    out = pl.pallas_call(
        functools.partial(transform_kernel, steps),
        out_shape=jax.ShapeDtypeStruct((GROUPS,) + tile, jnp.float32),
        in_specs=[smem, smem, hbm, hbm],
        out_specs=pl.BlockSpec(memory_space=pltpu.VMEM),
        scratch_shapes=[
            pltpu.VMEM((shells, width, occ), bf16),
            pltpu.VMEM(integrals.shape, bf16),
            pltpu.VMEM((2, occ // 8, 8, 4 * width), jnp.float32),
            pltpu.VMEM((2, occ, 4 * width), bf16),
            pltpu.VMEM((slots * width, occ), bf16),
            pltpu.VMEM((2, 2, 4 * width, 4 * width), bf16),
            pltpu.VMEM((GROUPS, 4, 2, 2) + tile, jnp.float32),
            pltpu.VMEM((GROUPS, 4, 2, 2) + tile, bf16),
            pltpu.VMEM((GROUPS, 4, 2, 2) + tile, bf16),
            pltpu.VMEM((GROUPS, 4, 2) + tile, bf16),
            pltpu.VMEM((GROUPS, 4, 2) + tile, bf16),
            pltpu.VMEM((GROUPS, 4) + tile, i16),
            pltpu.VMEM((GROUPS, 4) + tile, i16),
            pltpu.VMEM((GROUPS, 3) + tile, i16),
            pltpu.VMEM((GROUPS, 3) + tile, i16),
            pltpu.SemaphoreType.DMA((2,)),
            pltpu.SemaphoreType.DMA((GROUPS, 6)),
            pltpu.SemaphoreType.DMA((GROUPS, 6)),
        ],
        compiler_params=pltpu.CompilerParams(
            collective_id=0, has_side_effects=True, vmem_limit_bytes=60 * 1024 * 1024
        ),
    )(shell_pairs.T, block_count, coeffs.reshape(shells, width, occ), integrals)
    return out.reshape(kets, occ // 32, occ).transpose(1, 0, 2)


def on_device_general(integrals, coeffs, shell_pairs, block_count):
    slot_count = integrals.shape[0]
    shell_size = integrals.shape[1]
    ket_count = integrals.shape[2] // shell_size
    occ_count = coeffs.shape[1]
    shell_count = coeffs.shape[0] // shell_size
    pair_count = lax.axis_size("pair")
    red_count = lax.axis_size("red")
    pair_index = lax.axis_index("pair")
    red_index = lax.axis_index("red")
    owned_rows = occ_count // pair_count
    coef_table = coeffs.reshape(shell_count, shell_size, occ_count)
    first_slot = (pair_index * red_count + red_index) * slot_count
    own_pairs = lax.dynamic_slice_in_dim(shell_pairs, first_slot, slot_count, 0)
    live_mask = (jnp.arange(slot_count, dtype=jnp.int32) < block_count[0, 0]).astype(jnp.float32)
    left_panels = jnp.take(coef_table, own_pairs[:, 0], axis=0)
    half_done = jnp.einsum(
        "kmi,kmx->kix", left_panels, integrals, preferred_element_type=jnp.float32
    )
    half_done = (half_done * live_mask[:, None, None]).astype(jnp.bfloat16)
    right_panels = jnp.take(coef_table, own_pairs[:, 1], axis=0)
    whole_sum = jnp.einsum(
        "kpiqn,knrj->priqj",
        half_done.reshape(slot_count, pair_count, owned_rows, ket_count, shell_size),
        right_panels.reshape(slot_count, shell_size, red_count, occ_count // red_count),
        preferred_element_type=jnp.float32,
    )
    whole_sum = whole_sum.reshape(
        pair_count * red_count * owned_rows, ket_count, occ_count // red_count
    )
    return lax.psum_scatter(whole_sum, ("pair", "red"), scatter_dimension=0, tiled=True)


def solution(mesh):
    small = mesh.shape["pair"] == 32 and mesh.shape["red"] == 1
    return jax.shard_map(
        on_device if small else on_device_general,
        mesh=mesh,
        in_specs=(P(("pair", "red"), None, None), P(), P(), P("pair", "red")),
        out_specs=P("pair", None, "red"),
        check_vma=False,
    )
```

```python
import jax
import jax.numpy as jnp
from jax import lax
from jax.experimental import pallas as pl
from jax.experimental.pallas import tpu as pltpu
from jax.sharding import PartitionSpec as P

GROUPS = 12
LAGS = (1, 5, 9, 13)


def transform_kernel(
    pairs_ref, count_ref, coeffs_hbm, ints_hbm, out_ref,
    coeffs, ints, turned, left, right, diag,
    own, snd0, rcv0, snd1, rcv1, snd2, rcv2, snd3, rcv3,
    load_sem, send_sem, recv_sem,
):
    load_coeffs = pltpu.make_async_copy(coeffs_hbm, coeffs, load_sem.at[0])
    load_ints = pltpu.make_async_copy(ints_hbm, ints, load_sem.at[1])
    load_coeffs.start()
    load_ints.start()

    me = lax.axis_index("pair")

    def other(bit):
        return me + bit * (1 - 2 * ((me // bit) % 2))

    core_at, x_at, y_at = other(1), other(2), other(4)
    z_low, z_high = other(8) - me, other(16) - me
    z_at = (me + z_low, me + z_high, me + z_low + z_high)
    partners = (core_at, x_at, y_at) + z_at

    barrier = pltpu.get_barrier_semaphore()
    for at in partners:
        pl.semaphore_signal(
            barrier, inc=1, device_id={"pair": at}, device_id_type=pl.DeviceIdType.MESH
        )

    slots, width, columns = ints.shape
    occ = coeffs.shape[2]
    span = 4 * width
    diag[...] = jnp.zeros_like(diag)
    load_coeffs.wait()
    for k in range(slots):
        row_shell = pairs_ref[0, me * slots + k]
        col_shell = pairs_ref[1, me * slots + k]
        live = jnp.where(k < count_ref[0, 0], 1.0, 0.0).astype(jnp.float32)
        panel = coeffs[row_shell].astype(jnp.float32) * live
        turned[k // 4, :, :, pl.ds((k % 4) * width, width)] = panel.T.reshape(
            occ // 8, 8, width
        )
        right[pl.ds(k * width, width), :] = coeffs[col_shell]

    moves = [other(w) - me for w in (1, 2, 4, 8, 16)]

    def place(rel):
        at = me
        for n, move in enumerate(moves):
            if (rel >> n) % 2:
                at = at + move
        return at

    for core in range(2):
        for two in range(8):
            first = place(core + 2 * (2 * two))
            second = place(core + 2 * (2 * two + 1))
            for part in range(2):
                rows = jnp.concatenate([turned[part, first], turned[part, second]], axis=0)
                left[part, pl.ds(core * 128 + two * 16, 16), :] = rows.astype(jnp.bfloat16)

    load_ints.wait()

    lane = lax.broadcasted_iota(jnp.int32, (width, 2 * width), 1)
    low = lane < width
    per_group = columns // (2 * width) // GROUPS

    def compute(group):
        def one_pair(step, carry):
            cols = pl.ds(pl.multiple_of((group * per_group + step) * 2 * width, 2 * width), 2 * width)
            for k in range(slots):
                tile = ints[k, :, cols].astype(jnp.float32)
                swap = pltpu.roll(tile, width, 1)
                at_lane = pl.ds((k % 4) // 2 * 2 * width, 2 * width)
                at_row = pl.ds((k % 4) * width, width)
                for odd in range(2):
                    source = tile if k % 2 == odd else swap
                    keep = low if k % 2 == 0 else jnp.logical_not(low)
                    diag[odd, k // 4, at_row, at_lane] = jnp.where(keep, source, 0.0).astype(jnp.bfloat16)
            half = jnp.concatenate(
                [
                    jnp.concatenate(
                        [
                            jnp.dot(left[part], diag[odd, part], preferred_element_type=jnp.float32).astype(jnp.bfloat16)
                            for part in range(2)
                        ],
                        axis=1,
                    )
                    for odd in range(2)
                ],
                axis=0,
            )
            done = jnp.dot(half, right[...], preferred_element_type=jnp.float32)
            done = done.reshape(2, 2, 4, 2, 2, 8, occ)
            both = jnp.concatenate([done[0], done[1]], axis=4)
            own[group, :, :, :, step] = both[0]
            snd0[group, :, :, :, step] = both[1].astype(jnp.bfloat16)
            return carry

        lax.fori_loop(0, per_group, one_pair, 0)

    def copy(group, stage, source, target, at):
        return pltpu.make_async_remote_copy(
            src_ref=source,
            dst_ref=target,
            send_sem=send_sem.at[group, stage],
            recv_sem=recv_sem.at[group, stage],
            device_id={"pair": at},
            device_id_type=pl.DeviceIdType.MESH,
        )

    def core_copy(group):
        return copy(group, 0, snd0.at[group], rcv0.at[group], core_at)

    def first_copy(group, kind):
        at = y_at if kind else x_at
        return copy(group, 1, snd1.at[group], rcv1.at[group], at)

    def second_copy(group, kind):
        at = x_at if kind else y_at
        return copy(group, 2, snd2.at[group], rcv2.at[group], at)

    def z_copy(group, n):
        return copy(group, 3 + n, snd3.at[group, n], rcv3.at[group, n], z_at[n])

    def chunks(group, kind, z, a, b):
        y, x = (a, b) if kind == 0 else (b, a)
        return own[group, z, y, x] + rcv0[group, z, y, x].astype(jnp.float32)

    def stage1(group, kind):
        core_copy(group).wait_recv()
        snd1[group] = chunks(group, kind, slice(None), slice(None), 1).astype(jnp.bfloat16)
        first_copy(group, kind).start()

    def stage2(group, kind):
        first_copy(group, kind).wait_recv()
        total = chunks(group, kind, slice(None), 1, 0) + rcv1[group, :, 1].astype(jnp.float32)
        snd2[group] = total.astype(jnp.bfloat16)
        second_copy(group, kind).start()

    def gathered(group, kind, z):
        return (
            chunks(group, kind, z, 0, 0)
            + rcv1[group, z, 0].astype(jnp.float32)
            + rcv2[group, z].astype(jnp.float32)
        )

    def stage3(group, kind):
        second_copy(group, kind).wait_recv()
        for n in (1, 2, 0):
            snd3[group, n] = gathered(group, kind, n + 1).astype(jnp.bfloat16)
            z_copy(group, n).start()

    def finish(group, kind):
        total = gathered(group, kind, 0)
        for n in range(3):
            z_copy(group, n).wait_recv()
        total = total + jnp.sum(rcv3[group].astype(jnp.float32), axis=0)
        out_ref[group] = total

    stages = (stage1, stage2, stage3, finish)

    def two_ticks(turn, carry):
        for kind in range(2):
            tick = 2 * turn + kind

            @pl.when(tick < GROUPS)
            def _():
                compute(tick)
                if kind == 0:
                    @pl.when(turn == 0)
                    def _():
                        pl.semaphore_wait(barrier, len(partners))
                core_copy(tick).start()

            for lag, stage in zip(LAGS, stages):
                group = tick - lag

                @pl.when(jnp.logical_and(group >= 0, group < GROUPS))
                def _(group=group, stage=stage):
                    stage(group, 1 - kind)
        return carry

    lax.fori_loop(0, (GROUPS + LAGS[-1] + 1) // 2, two_ticks, 0)

    def drain(half, carry):
        for kind in range(2):
            group = 2 * half + kind
            core_copy(group).wait_send()
            first_copy(group, kind).wait_send()
            second_copy(group, kind).wait_send()
            for n in range(3):
                z_copy(group, n).wait_send()
        return carry

    lax.fori_loop(0, GROUPS // 2, drain, 0)


def on_device(integrals, coeffs, shell_pairs, block_count):
    slots, width, columns = integrals.shape
    occ = coeffs.shape[1]
    kets = columns // width
    shells = coeffs.shape[0] // width
    per_group = kets // 2 // GROUPS
    tile = (per_group, 16, occ)
    bf16 = jnp.bfloat16
    hbm = pl.BlockSpec(memory_space=pltpu.HBM)
    smem = pl.BlockSpec(memory_space=pltpu.SMEM)
    out = pl.pallas_call(
        transform_kernel,
        out_shape=jax.ShapeDtypeStruct((GROUPS,) + tile, jnp.float32),
        in_specs=[smem, smem, hbm, hbm],
        out_specs=pl.BlockSpec(memory_space=pltpu.VMEM),
        scratch_shapes=[
            pltpu.VMEM((shells, width, occ), bf16),
            pltpu.VMEM(integrals.shape, bf16),
            pltpu.VMEM((2, occ // 8, 8, 4 * width), jnp.float32),
            pltpu.VMEM((2, occ, 4 * width), bf16),
            pltpu.VMEM((slots * width, occ), bf16),
            pltpu.VMEM((2, 2, 4 * width, 4 * width), bf16),
            pltpu.VMEM((GROUPS, 4, 2, 2) + tile, jnp.float32),
            pltpu.VMEM((GROUPS, 4, 2, 2) + tile, bf16),
            pltpu.VMEM((GROUPS, 4, 2, 2) + tile, bf16),
            pltpu.VMEM((GROUPS, 4, 2) + tile, bf16),
            pltpu.VMEM((GROUPS, 4, 2) + tile, bf16),
            pltpu.VMEM((GROUPS, 4) + tile, bf16),
            pltpu.VMEM((GROUPS, 4) + tile, bf16),
            pltpu.VMEM((GROUPS, 3) + tile, bf16),
            pltpu.VMEM((GROUPS, 3) + tile, bf16),
            pltpu.SemaphoreType.DMA((2,)),
            pltpu.SemaphoreType.DMA((GROUPS, 6)),
            pltpu.SemaphoreType.DMA((GROUPS, 6)),
        ],
        compiler_params=pltpu.CompilerParams(
            collective_id=0, has_side_effects=True, vmem_limit_bytes=53 * 1024 * 1024
        ),
    )(shell_pairs.T, block_count, coeffs.reshape(shells, width, occ), integrals)
    return out.reshape(kets, occ // 32, occ).transpose(1, 0, 2)


def on_device_general(integrals, coeffs, shell_pairs, block_count):
    slot_count = integrals.shape[0]
    shell_size = integrals.shape[1]
    ket_count = integrals.shape[2] // shell_size
    occ_count = coeffs.shape[1]
    shell_count = coeffs.shape[0] // shell_size
    pair_count = lax.axis_size("pair")
    red_count = lax.axis_size("red")
    pair_index = lax.axis_index("pair")
    red_index = lax.axis_index("red")
    owned_rows = occ_count // pair_count
    coef_table = coeffs.reshape(shell_count, shell_size, occ_count)
    first_slot = (pair_index * red_count + red_index) * slot_count
    own_pairs = lax.dynamic_slice_in_dim(shell_pairs, first_slot, slot_count, 0)
    live_mask = (jnp.arange(slot_count, dtype=jnp.int32) < block_count[0, 0]).astype(jnp.float32)
    left_panels = jnp.take(coef_table, own_pairs[:, 0], axis=0)
    half_done = jnp.einsum(
        "kmi,kmx->kix", left_panels, integrals, preferred_element_type=jnp.float32
    )
    half_done = (half_done * live_mask[:, None, None]).astype(jnp.bfloat16)
    right_panels = jnp.take(coef_table, own_pairs[:, 1], axis=0)
    whole_sum = jnp.einsum(
        "kpiqn,knrj->priqj",
        half_done.reshape(slot_count, pair_count, owned_rows, ket_count, shell_size),
        right_panels.reshape(slot_count, shell_size, red_count, occ_count // red_count),
        preferred_element_type=jnp.float32,
    )
    whole_sum = whole_sum.reshape(
        pair_count * red_count * owned_rows, ket_count, occ_count // red_count
    )
    return lax.psum_scatter(whole_sum, ("pair", "red"), scatter_dimension=0, tiled=True)


def solution(mesh):
    small = mesh.shape["pair"] == 32 and mesh.shape["red"] == 1
    return jax.shard_map(
        on_device if small else on_device_general,
        mesh=mesh,
        in_specs=(P(("pair", "red"), None, None), P(), P(), P("pair", "red")),
        out_specs=P("pair", None, "red"),
        check_vma=False,
    )
```

```python
import jax
import jax.numpy as jnp
from jax import lax
from jax.experimental import pallas as pl
from jax.experimental.pallas import tpu as pltpu
from jax.sharding import PartitionSpec as P

GROUPS = 12
LAGS = (3, 7, 11, 15)


def transform_kernel(
    pairs_ref, count_ref, coeffs_hbm, ints_hbm, out_ref,
    coeffs, ints, turned, left, right, diag,
    own, snd0, rcv0, snd1, rcv1, snd2, rcv2, snd3, rcv3,
    load_sem, send_sem, recv_sem,
):
    load_coeffs = pltpu.make_async_copy(coeffs_hbm, coeffs, load_sem.at[0])
    load_ints = pltpu.make_async_copy(ints_hbm, ints, load_sem.at[1])
    load_coeffs.start()
    load_ints.start()

    me = lax.axis_index("pair")

    def other(bit):
        return me + bit * (1 - 2 * ((me // bit) % 2))

    core_at, x_at, y_at = other(1), other(2), other(4)
    z_low, z_high = other(8) - me, other(16) - me
    z_at = (me + z_low, me + z_high, me + z_low + z_high)
    partners = (core_at, x_at, y_at) + z_at

    barrier = pltpu.get_barrier_semaphore()
    for at in partners:
        pl.semaphore_signal(
            barrier, inc=1, device_id={"pair": at}, device_id_type=pl.DeviceIdType.MESH
        )

    slots, width, columns = ints.shape
    occ = coeffs.shape[2]
    span = 4 * width
    diag[...] = jnp.zeros_like(diag)
    load_coeffs.wait()
    for k in range(slots):
        row_shell = pairs_ref[0, me * slots + k]
        col_shell = pairs_ref[1, me * slots + k]
        live = jnp.where(k < count_ref[0, 0], 1.0, 0.0).astype(jnp.float32)
        panel = coeffs[row_shell].astype(jnp.float32) * live
        turned[k // 4, :, :, pl.ds((k % 4) * width, width)] = panel.T.reshape(
            occ // 8, 8, width
        )
        right[pl.ds(k * width, width), :] = coeffs[col_shell]

    moves = [other(w) - me for w in (1, 2, 4, 8, 16)]

    def place(rel):
        at = me
        for n, move in enumerate(moves):
            if (rel >> n) % 2:
                at = at + move
        return at

    for core in range(2):
        for two in range(8):
            first = place(core + 2 * (2 * two))
            second = place(core + 2 * (2 * two + 1))
            for part in range(2):
                rows = jnp.concatenate([turned[part, first], turned[part, second]], axis=0)
                left[part, pl.ds(core * 128 + two * 16, 16), :] = rows.astype(jnp.bfloat16)

    load_ints.wait()

    lane = lax.broadcasted_iota(jnp.int32, (width, 2 * width), 1)
    low = lane < width
    per_group = columns // (2 * width) // GROUPS

    def compute(group):
        def one_pair(step, carry):
            cols = pl.ds(pl.multiple_of((group * per_group + step) * 2 * width, 2 * width), 2 * width)
            for k in range(slots):
                tile = ints[k, :, cols].astype(jnp.float32)
                swap = pltpu.roll(tile, width, 1)
                at_lane = pl.ds((k % 4) // 2 * 2 * width, 2 * width)
                at_row = pl.ds((k % 4) * width, width)
                for odd in range(2):
                    source = tile if k % 2 == odd else swap
                    keep = low if k % 2 == 0 else jnp.logical_not(low)
                    diag[odd, k // 4, at_row, at_lane] = jnp.where(keep, source, 0.0).astype(jnp.bfloat16)
            half = jnp.concatenate(
                [
                    jnp.concatenate(
                        [
                            jnp.dot(left[part], diag[odd, part], preferred_element_type=jnp.float32).astype(jnp.bfloat16)
                            for part in range(2)
                        ],
                        axis=1,
                    )
                    for odd in range(2)
                ],
                axis=0,
            )
            done = jnp.dot(half, right[...], preferred_element_type=jnp.float32)
            done = done.reshape(2, 2, 4, 2, 2, 8, occ)
            both = jnp.concatenate([done[0], done[1]], axis=4)
            own[group, :, :, :, step] = both[0]
            snd0[group, :, :, :, step] = both[1].astype(jnp.bfloat16)
            return carry

        lax.fori_loop(0, per_group, one_pair, 0)

    def copy(group, stage, source, target, at):
        return pltpu.make_async_remote_copy(
            src_ref=source,
            dst_ref=target,
            send_sem=send_sem.at[group, stage],
            recv_sem=recv_sem.at[group, stage],
            device_id={"pair": at},
            device_id_type=pl.DeviceIdType.MESH,
        )

    def core_copy(group):
        return copy(group, 0, snd0.at[group], rcv0.at[group], core_at)

    def first_copy(group, kind):
        at = y_at if kind else x_at
        return copy(group, 1, snd1.at[group], rcv1.at[group], at)

    def second_copy(group, kind):
        at = x_at if kind else y_at
        return copy(group, 2, snd2.at[group], rcv2.at[group], at)

    def z_copy(group, n):
        return copy(group, 3 + n, snd3.at[group, n], rcv3.at[group, n], z_at[n])

    def chunks(group, kind, z, a, b):
        y, x = (a, b) if kind == 0 else (b, a)
        return own[group, z, y, x] + rcv0[group, z, y, x].astype(jnp.float32)

    def stage1(group, kind):
        core_copy(group).wait_recv()
        snd1[group] = chunks(group, kind, slice(None), slice(None), 1).astype(jnp.bfloat16)
        first_copy(group, kind).start()

    def stage2(group, kind):
        first_copy(group, kind).wait_recv()
        total = chunks(group, kind, slice(None), 1, 0) + rcv1[group, :, 1].astype(jnp.float32)
        snd2[group] = total.astype(jnp.bfloat16)
        second_copy(group, kind).start()

    def gathered(group, kind, z):
        return (
            chunks(group, kind, z, 0, 0)
            + rcv1[group, z, 0].astype(jnp.float32)
            + rcv2[group, z].astype(jnp.float32)
        )

    def stage3(group, kind):
        second_copy(group, kind).wait_recv()
        for n in (1, 2, 0):
            snd3[group, n] = gathered(group, kind, n + 1).astype(jnp.bfloat16)
            z_copy(group, n).start()

    def finish(group, kind):
        total = gathered(group, kind, 0)
        for n in range(3):
            z_copy(group, n).wait_recv()
        total = total + jnp.sum(rcv3[group].astype(jnp.float32), axis=0)
        out_ref[group] = total

    stages = (stage1, stage2, stage3, finish)

    def two_ticks(turn, carry):
        for kind in range(2):
            tick = 2 * turn + kind

            @pl.when(tick < GROUPS)
            def _():
                compute(tick)
                if kind == 0:
                    @pl.when(turn == 0)
                    def _():
                        pl.semaphore_wait(barrier, len(partners))
                core_copy(tick).start()

            for lag, stage in zip(LAGS, stages):
                group = tick - lag

                @pl.when(jnp.logical_and(group >= 0, group < GROUPS))
                def _(group=group, stage=stage):
                    stage(group, 1 - kind)
        return carry

    lax.fori_loop(0, (GROUPS + LAGS[-1] + 1) // 2, two_ticks, 0)

    def drain(half, carry):
        for kind in range(2):
            group = 2 * half + kind
            core_copy(group).wait_send()
            first_copy(group, kind).wait_send()
            second_copy(group, kind).wait_send()
            for n in range(3):
                z_copy(group, n).wait_send()
        return carry

    lax.fori_loop(0, GROUPS // 2, drain, 0)


def on_device(integrals, coeffs, shell_pairs, block_count):
    slots, width, columns = integrals.shape
    occ = coeffs.shape[1]
    kets = columns // width
    shells = coeffs.shape[0] // width
    per_group = kets // 2 // GROUPS
    tile = (per_group, 16, occ)
    bf16 = jnp.bfloat16
    hbm = pl.BlockSpec(memory_space=pltpu.HBM)
    smem = pl.BlockSpec(memory_space=pltpu.SMEM)
    out = pl.pallas_call(
        transform_kernel,
        out_shape=jax.ShapeDtypeStruct((GROUPS,) + tile, jnp.float32),
        in_specs=[smem, smem, hbm, hbm],
        out_specs=pl.BlockSpec(memory_space=pltpu.VMEM),
        scratch_shapes=[
            pltpu.VMEM((shells, width, occ), bf16),
            pltpu.VMEM(integrals.shape, bf16),
            pltpu.VMEM((2, occ // 8, 8, 4 * width), jnp.float32),
            pltpu.VMEM((2, occ, 4 * width), bf16),
            pltpu.VMEM((slots * width, occ), bf16),
            pltpu.VMEM((2, 2, 4 * width, 4 * width), bf16),
            pltpu.VMEM((GROUPS, 4, 2, 2) + tile, jnp.float32),
            pltpu.VMEM((GROUPS, 4, 2, 2) + tile, bf16),
            pltpu.VMEM((GROUPS, 4, 2, 2) + tile, bf16),
            pltpu.VMEM((GROUPS, 4, 2) + tile, bf16),
            pltpu.VMEM((GROUPS, 4, 2) + tile, bf16),
            pltpu.VMEM((GROUPS, 4) + tile, bf16),
            pltpu.VMEM((GROUPS, 4) + tile, bf16),
            pltpu.VMEM((GROUPS, 3) + tile, bf16),
            pltpu.VMEM((GROUPS, 3) + tile, bf16),
            pltpu.SemaphoreType.DMA((2,)),
            pltpu.SemaphoreType.DMA((GROUPS, 6)),
            pltpu.SemaphoreType.DMA((GROUPS, 6)),
        ],
        compiler_params=pltpu.CompilerParams(
            collective_id=0, has_side_effects=True, vmem_limit_bytes=53 * 1024 * 1024
        ),
    )(shell_pairs.T, block_count, coeffs.reshape(shells, width, occ), integrals)
    return out.reshape(kets, occ // 32, occ).transpose(1, 0, 2)


def on_device_general(integrals, coeffs, shell_pairs, block_count):
    slot_count = integrals.shape[0]
    shell_size = integrals.shape[1]
    ket_count = integrals.shape[2] // shell_size
    occ_count = coeffs.shape[1]
    shell_count = coeffs.shape[0] // shell_size
    pair_count = lax.axis_size("pair")
    red_count = lax.axis_size("red")
    pair_index = lax.axis_index("pair")
    red_index = lax.axis_index("red")
    owned_rows = occ_count // pair_count
    coef_table = coeffs.reshape(shell_count, shell_size, occ_count)
    first_slot = (pair_index * red_count + red_index) * slot_count
    own_pairs = lax.dynamic_slice_in_dim(shell_pairs, first_slot, slot_count, 0)
    live_mask = (jnp.arange(slot_count, dtype=jnp.int32) < block_count[0, 0]).astype(jnp.float32)
    left_panels = jnp.take(coef_table, own_pairs[:, 0], axis=0)
    half_done = jnp.einsum(
        "kmi,kmx->kix", left_panels, integrals, preferred_element_type=jnp.float32
    )
    half_done = (half_done * live_mask[:, None, None]).astype(jnp.bfloat16)
    right_panels = jnp.take(coef_table, own_pairs[:, 1], axis=0)
    whole_sum = jnp.einsum(
        "kpiqn,knrj->priqj",
        half_done.reshape(slot_count, pair_count, owned_rows, ket_count, shell_size),
        right_panels.reshape(slot_count, shell_size, red_count, occ_count // red_count),
        preferred_element_type=jnp.float32,
    )
    whole_sum = whole_sum.reshape(
        pair_count * red_count * owned_rows, ket_count, occ_count // red_count
    )
    return lax.psum_scatter(whole_sum, ("pair", "red"), scatter_dimension=0, tiled=True)


def solution(mesh):
    small = mesh.shape["pair"] == 32 and mesh.shape["red"] == 1
    return jax.shard_map(
        on_device if small else on_device_general,
        mesh=mesh,
        in_specs=(P(("pair", "red"), None, None), P(), P(), P("pair", "red")),
        out_specs=P("pair", None, "red"),
        check_vma=False,
    )
```

```python
import jax
import jax.numpy as jnp
from jax import lax
from jax.experimental import pallas as pl
from jax.experimental.pallas import tpu as pltpu
from jax.sharding import PartitionSpec as P

GROUPS = 12
COEFF_LOADS = 6
INT_LOADS = 3
LAGS = (3, 7, 11, 15)


def transform_kernel(
    pairs_ref, count_ref, coeffs_hbm, ints_hbm, out_ref,
    coeffs, ints, turned, left, right, diag,
    own, snd0, rcv0, snd1, rcv1, snd2, rcv2, snd3, rcv3,
    load_sem, send_sem, recv_sem,
):
    shells = coeffs.shape[0]
    share = -(-shells // COEFF_LOADS)
    load_coeffs = []
    for n in range(COEFF_LOADS):
        part = pl.ds(n * share, min(share, shells - n * share))
        load_coeffs.append(
            pltpu.make_async_copy(coeffs_hbm.at[part], coeffs.at[part], load_sem.at[n])
        )
    wide = ints.shape[2] // INT_LOADS

    def load_ints(n):
        part = pl.ds(pl.multiple_of(n * wide, wide), wide)
        return pltpu.make_async_copy(
            ints_hbm.at[:, :, part], ints.at[:, :, part], load_sem.at[COEFF_LOADS + n]
        )

    for item in load_coeffs:
        item.start()
    for n in range(INT_LOADS):
        load_ints(n).start()

    me = lax.axis_index("pair")

    def other(bit):
        return me + bit * (1 - 2 * ((me // bit) % 2))

    core_at, x_at, y_at = other(1), other(2), other(4)
    z_low, z_high = other(8) - me, other(16) - me
    z_at = (me + z_low, me + z_high, me + z_low + z_high)
    partners = (core_at, x_at, y_at) + z_at

    barrier = pltpu.get_barrier_semaphore()
    for at in partners:
        pl.semaphore_signal(
            barrier, inc=1, device_id={"pair": at}, device_id_type=pl.DeviceIdType.MESH
        )

    slots, width, columns = ints.shape
    occ = coeffs.shape[2]
    span = 4 * width
    diag[...] = jnp.zeros_like(diag)
    for item in load_coeffs:
        item.wait()
    for k in range(slots):
        row_shell = pairs_ref[0, me * slots + k]
        col_shell = pairs_ref[1, me * slots + k]
        live = jnp.where(k < count_ref[0, 0], 1.0, 0.0).astype(jnp.float32)
        panel = coeffs[row_shell].astype(jnp.float32) * live
        turned[k // 4, :, :, pl.ds((k % 4) * width, width)] = panel.T.reshape(
            occ // 8, 8, width
        )
        right[pl.ds(k * width, width), :] = coeffs[col_shell]

    moves = [other(w) - me for w in (1, 2, 4, 8, 16)]

    def place(rel):
        at = me
        for n, move in enumerate(moves):
            if (rel >> n) % 2:
                at = at + move
        return at

    for core in range(2):
        for two in range(8):
            first = place(core + 2 * (2 * two))
            second = place(core + 2 * (2 * two + 1))
            for part in range(2):
                rows = jnp.concatenate([turned[part, first], turned[part, second]], axis=0)
                left[part, pl.ds(core * 128 + two * 16, 16), :] = rows.astype(jnp.bfloat16)

    lane = lax.broadcasted_iota(jnp.int32, (width, 2 * width), 1)
    low = lane < width
    per_group = columns // (2 * width) // GROUPS

    def compute(group):
        def one_pair(step, carry):
            cols = pl.ds(pl.multiple_of((group * per_group + step) * 2 * width, 2 * width), 2 * width)
            for k in range(slots):
                tile = ints[k, :, cols].astype(jnp.float32)
                swap = pltpu.roll(tile, width, 1)
                at_lane = pl.ds((k % 4) // 2 * 2 * width, 2 * width)
                at_row = pl.ds((k % 4) * width, width)
                for odd in range(2):
                    source = tile if k % 2 == odd else swap
                    keep = low if k % 2 == 0 else jnp.logical_not(low)
                    diag[odd, k // 4, at_row, at_lane] = jnp.where(keep, source, 0.0).astype(jnp.bfloat16)
            half = jnp.concatenate(
                [
                    jnp.concatenate(
                        [
                            jnp.dot(left[part], diag[odd, part], preferred_element_type=jnp.float32).astype(jnp.bfloat16)
                            for part in range(2)
                        ],
                        axis=1,
                    )
                    for odd in range(2)
                ],
                axis=0,
            )
            done = jnp.dot(half, right[...], preferred_element_type=jnp.float32)
            done = done.reshape(2, 2, 4, 2, 2, 8, occ)
            both = jnp.concatenate([done[0], done[1]], axis=4)
            own[group, :, :, :, step] = both[0]
            snd0[group, :, :, :, step] = both[1].astype(jnp.bfloat16)
            return carry

        lax.fori_loop(0, per_group, one_pair, 0)

    def copy(group, stage, source, target, at):
        return pltpu.make_async_remote_copy(
            src_ref=source,
            dst_ref=target,
            send_sem=send_sem.at[group, stage],
            recv_sem=recv_sem.at[group, stage],
            device_id={"pair": at},
            device_id_type=pl.DeviceIdType.MESH,
        )

    def core_copy(group):
        return copy(group, 0, snd0.at[group], rcv0.at[group], core_at)

    def first_copy(group, kind):
        at = y_at if kind else x_at
        return copy(group, 1, snd1.at[group], rcv1.at[group], at)

    def second_copy(group, kind):
        at = x_at if kind else y_at
        return copy(group, 2, snd2.at[group], rcv2.at[group], at)

    def z_copy(group, n):
        return copy(group, 3 + n, snd3.at[group, n], rcv3.at[group, n], z_at[n])

    def chunks(group, kind, z, a, b):
        y, x = (a, b) if kind == 0 else (b, a)
        return own[group, z, y, x] + rcv0[group, z, y, x].astype(jnp.float32)

    def stage1(group, kind):
        core_copy(group).wait_recv()
        snd1[group] = chunks(group, kind, slice(None), slice(None), 1).astype(jnp.bfloat16)
        first_copy(group, kind).start()

    def stage2(group, kind):
        first_copy(group, kind).wait_recv()
        total = chunks(group, kind, slice(None), 1, 0) + rcv1[group, :, 1].astype(jnp.float32)
        snd2[group] = total.astype(jnp.bfloat16)
        second_copy(group, kind).start()

    def gathered(group, kind, z):
        return (
            chunks(group, kind, z, 0, 0)
            + rcv1[group, z, 0].astype(jnp.float32)
            + rcv2[group, z].astype(jnp.float32)
        )

    def stage3(group, kind):
        second_copy(group, kind).wait_recv()
        for n in (1, 2, 0):
            snd3[group, n] = gathered(group, kind, n + 1).astype(jnp.bfloat16)
            z_copy(group, n).start()

    def finish(group, kind):
        total = gathered(group, kind, 0)
        for n in range(3):
            z_copy(group, n).wait_recv()
        total = total + jnp.sum(rcv3[group].astype(jnp.float32), axis=0)
        out_ref[group] = total

    stages = (stage1, stage2, stage3, finish)

    def two_ticks(turn, carry):
        for kind in range(2):
            tick = 2 * turn + kind

            @pl.when(tick < GROUPS)
            def _():
                if kind == 0:
                    @pl.when(turn % (GROUPS // INT_LOADS // 2) == 0)
                    def _():
                        load_ints(turn // (GROUPS // INT_LOADS // 2)).wait()
                compute(tick)
                if kind == 0:
                    @pl.when(turn == 0)
                    def _():
                        pl.semaphore_wait(barrier, len(partners))
                core_copy(tick).start()

            for lag, stage in zip(LAGS, stages):
                group = tick - lag

                @pl.when(jnp.logical_and(group >= 0, group < GROUPS))
                def _(group=group, stage=stage):
                    stage(group, 1 - kind)
        return carry

    lax.fori_loop(0, (GROUPS + LAGS[-1] + 1) // 2, two_ticks, 0)

    def drain(half, carry):
        for kind in range(2):
            group = 2 * half + kind
            core_copy(group).wait_send()
            first_copy(group, kind).wait_send()
            second_copy(group, kind).wait_send()
            for n in range(3):
                z_copy(group, n).wait_send()
        return carry

    lax.fori_loop(0, GROUPS // 2, drain, 0)


def on_device(integrals, coeffs, shell_pairs, block_count):
    slots, width, columns = integrals.shape
    occ = coeffs.shape[1]
    kets = columns // width
    shells = coeffs.shape[0] // width
    per_group = kets // 2 // GROUPS
    tile = (per_group, 16, occ)
    bf16 = jnp.bfloat16
    hbm = pl.BlockSpec(memory_space=pltpu.HBM)
    smem = pl.BlockSpec(memory_space=pltpu.SMEM)
    out = pl.pallas_call(
        transform_kernel,
        out_shape=jax.ShapeDtypeStruct((GROUPS,) + tile, jnp.float32),
        in_specs=[smem, smem, hbm, hbm],
        out_specs=pl.BlockSpec(memory_space=pltpu.VMEM),
        scratch_shapes=[
            pltpu.VMEM((shells, width, occ), bf16),
            pltpu.VMEM(integrals.shape, bf16),
            pltpu.VMEM((2, occ // 8, 8, 4 * width), jnp.float32),
            pltpu.VMEM((2, occ, 4 * width), bf16),
            pltpu.VMEM((slots * width, occ), bf16),
            pltpu.VMEM((2, 2, 4 * width, 4 * width), bf16),
            pltpu.VMEM((GROUPS, 4, 2, 2) + tile, jnp.float32),
            pltpu.VMEM((GROUPS, 4, 2, 2) + tile, bf16),
            pltpu.VMEM((GROUPS, 4, 2, 2) + tile, bf16),
            pltpu.VMEM((GROUPS, 4, 2) + tile, bf16),
            pltpu.VMEM((GROUPS, 4, 2) + tile, bf16),
            pltpu.VMEM((GROUPS, 4) + tile, bf16),
            pltpu.VMEM((GROUPS, 4) + tile, bf16),
            pltpu.VMEM((GROUPS, 3) + tile, bf16),
            pltpu.VMEM((GROUPS, 3) + tile, bf16),
            pltpu.SemaphoreType.DMA((COEFF_LOADS + INT_LOADS,)),
            pltpu.SemaphoreType.DMA((GROUPS, 6)),
            pltpu.SemaphoreType.DMA((GROUPS, 6)),
        ],
        compiler_params=pltpu.CompilerParams(
            collective_id=0, has_side_effects=True, vmem_limit_bytes=53 * 1024 * 1024
        ),
    )(shell_pairs.T, block_count, coeffs.reshape(shells, width, occ), integrals)
    return out.reshape(kets, occ // 32, occ).transpose(1, 0, 2)


def on_device_general(integrals, coeffs, shell_pairs, block_count):
    slot_count = integrals.shape[0]
    shell_size = integrals.shape[1]
    ket_count = integrals.shape[2] // shell_size
    occ_count = coeffs.shape[1]
    shell_count = coeffs.shape[0] // shell_size
    pair_count = lax.axis_size("pair")
    red_count = lax.axis_size("red")
    pair_index = lax.axis_index("pair")
    red_index = lax.axis_index("red")
    owned_rows = occ_count // pair_count
    coef_table = coeffs.reshape(shell_count, shell_size, occ_count)
    first_slot = (pair_index * red_count + red_index) * slot_count
    own_pairs = lax.dynamic_slice_in_dim(shell_pairs, first_slot, slot_count, 0)
    live_mask = (jnp.arange(slot_count, dtype=jnp.int32) < block_count[0, 0]).astype(jnp.float32)
    left_panels = jnp.take(coef_table, own_pairs[:, 0], axis=0)
    half_done = jnp.einsum(
        "kmi,kmx->kix", left_panels, integrals, preferred_element_type=jnp.float32
    )
    half_done = (half_done * live_mask[:, None, None]).astype(jnp.bfloat16)
    right_panels = jnp.take(coef_table, own_pairs[:, 1], axis=0)
    whole_sum = jnp.einsum(
        "kpiqn,knrj->priqj",
        half_done.reshape(slot_count, pair_count, owned_rows, ket_count, shell_size),
        right_panels.reshape(slot_count, shell_size, red_count, occ_count // red_count),
        preferred_element_type=jnp.float32,
    )
    whole_sum = whole_sum.reshape(
        pair_count * red_count * owned_rows, ket_count, occ_count // red_count
    )
    return lax.psum_scatter(whole_sum, ("pair", "red"), scatter_dimension=0, tiled=True)


def solution(mesh):
    small = mesh.shape["pair"] == 32 and mesh.shape["red"] == 1
    return jax.shard_map(
        on_device if small else on_device_general,
        mesh=mesh,
        in_specs=(P(("pair", "red"), None, None), P(), P(), P("pair", "red")),
        out_specs=P("pair", None, "red"),
        check_vma=False,
    )
```

```python
import jax
import jax.numpy as jnp
from jax import lax
from jax.experimental import pallas as pl
from jax.experimental.pallas import tpu as pltpu
from jax.sharding import PartitionSpec as P

GROUPS = 12
LAGS = (3, 7, 11, 15)


def transform_kernel(
    pairs_ref, count_ref, coeffs_hbm, ints_hbm, out_ref,
    coeffs, ints, turned, left, right, diag, half,
    own, snd0, rcv0, snd1, rcv1, snd2, rcv2, snd3, rcv3,
    load_sem, send_sem, recv_sem,
):
    load_coeffs = pltpu.make_async_copy(coeffs_hbm, coeffs, load_sem.at[0])
    load_ints = pltpu.make_async_copy(ints_hbm, ints, load_sem.at[1])
    load_coeffs.start()
    load_ints.start()

    me = lax.axis_index("pair")

    def other(bit):
        return me + bit * (1 - 2 * ((me // bit) % 2))

    core_at, x_at, y_at = other(1), other(2), other(4)
    z_low, z_high = other(8) - me, other(16) - me
    z_at = (me + z_low, me + z_high, me + z_low + z_high)
    partners = (core_at, x_at, y_at) + z_at

    barrier = pltpu.get_barrier_semaphore()
    for at in partners:
        pl.semaphore_signal(
            barrier, inc=1, device_id={"pair": at}, device_id_type=pl.DeviceIdType.MESH
        )

    slots, width, columns = ints.shape
    occ = coeffs.shape[2]
    span = 4 * width
    diag[...] = jnp.zeros_like(diag)
    load_coeffs.wait()
    for k in range(slots):
        row_shell = pairs_ref[0, me * slots + k]
        col_shell = pairs_ref[1, me * slots + k]
        live = jnp.where(k < count_ref[0, 0], 1.0, 0.0).astype(jnp.float32)
        panel = coeffs[row_shell].astype(jnp.float32) * live
        turned[k // 4, :, :, pl.ds((k % 4) * width, width)] = panel.T.reshape(
            occ // 8, 8, width
        )
        right[pl.ds(k * width, width), :] = coeffs[col_shell]

    moves = [other(w) - me for w in (1, 2, 4, 8, 16)]

    def place(rel):
        at = me
        for n, move in enumerate(moves):
            if (rel >> n) % 2:
                at = at + move
        return at

    for core in range(2):
        for two in range(8):
            first = place(core + 2 * (2 * two))
            second = place(core + 2 * (2 * two + 1))
            for part in range(2):
                rows = jnp.concatenate([turned[part, first], turned[part, second]], axis=0)
                left[part, pl.ds(core * 128 + two * 16, 16), :] = rows.astype(jnp.bfloat16)

    load_ints.wait()

    lane = lax.broadcasted_iota(jnp.int32, (width, 2 * width), 1)
    low = lane < width

    def lay_out(group, kind):
        cols = pl.ds(pl.multiple_of(group * 2 * width, 2 * width), 2 * width)
        for k in range(slots):
            tile = ints[k, :, cols].astype(jnp.float32)
            swap = pltpu.roll(tile, width, 1)
            at_lane = pl.ds((k % 4) // 2 * 2 * width, 2 * width)
            at_row = pl.ds((k % 4) * width, width)
            for odd in range(2):
                source = tile if k % 2 == odd else swap
                keep = low if k % 2 == 0 else jnp.logical_not(low)
                diag[kind, odd, k // 4, at_row, at_lane] = jnp.where(keep, source, 0.0).astype(jnp.bfloat16)

    def first_half(kind):
        for odd in range(2):
            for part in range(2):
                product = jnp.dot(left[part], diag[kind, odd, part], preferred_element_type=jnp.float32)
                half[kind, pl.ds(odd * occ, occ), pl.ds(part * span, span)] = product.astype(jnp.bfloat16)

    def second_half(group, kind):
        done = jnp.dot(half[kind], right[...], preferred_element_type=jnp.float32)
        done = done.reshape(2, 2, 4, 2, 2, 8, occ)
        both = jnp.concatenate([done[0], done[1]], axis=4)
        own[group] = both[0]
        snd0[group] = both[1].astype(jnp.bfloat16)

    def compute(group, kind):
        second_half(group, kind)
        first_half(1 - kind)
        lay_out((group + 2) % GROUPS, kind)

    lay_out(0, 0)
    first_half(0)
    lay_out(1, 1)

    def copy(group, stage, source, target, at):
        return pltpu.make_async_remote_copy(
            src_ref=source,
            dst_ref=target,
            send_sem=send_sem.at[group, stage],
            recv_sem=recv_sem.at[group, stage],
            device_id={"pair": at},
            device_id_type=pl.DeviceIdType.MESH,
        )

    def core_copy(group):
        return copy(group, 0, snd0.at[group], rcv0.at[group], core_at)

    def first_copy(group, kind):
        at = y_at if kind else x_at
        return copy(group, 1, snd1.at[group], rcv1.at[group], at)

    def second_copy(group, kind):
        at = x_at if kind else y_at
        return copy(group, 2, snd2.at[group], rcv2.at[group], at)

    def z_copy(group, n):
        return copy(group, 3 + n, snd3.at[group, n], rcv3.at[group, n], z_at[n])

    def chunks(group, kind, z, a, b):
        y, x = (a, b) if kind == 0 else (b, a)
        return own[group, z, y, x] + rcv0[group, z, y, x].astype(jnp.float32)

    def stage1(group, kind):
        core_copy(group).wait_recv()
        snd1[group] = chunks(group, kind, slice(None), slice(None), 1).astype(jnp.bfloat16)
        first_copy(group, kind).start()

    def stage2(group, kind):
        first_copy(group, kind).wait_recv()
        total = chunks(group, kind, slice(None), 1, 0) + rcv1[group, :, 1].astype(jnp.float32)
        snd2[group] = total.astype(jnp.bfloat16)
        second_copy(group, kind).start()

    def gathered(group, kind, z):
        return (
            chunks(group, kind, z, 0, 0)
            + rcv1[group, z, 0].astype(jnp.float32)
            + rcv2[group, z].astype(jnp.float32)
        )

    def stage3(group, kind):
        second_copy(group, kind).wait_recv()
        for n in (1, 2, 0):
            snd3[group, n] = gathered(group, kind, n + 1).astype(jnp.bfloat16)
            z_copy(group, n).start()

    def finish(group, kind):
        total = gathered(group, kind, 0)
        for n in range(3):
            z_copy(group, n).wait_recv()
        total = total + jnp.sum(rcv3[group].astype(jnp.float32), axis=0)
        out_ref[group] = total

    stages = (stage1, stage2, stage3, finish)

    def two_ticks(turn, carry):
        for kind in range(2):
            tick = 2 * turn + kind

            @pl.when(tick < GROUPS)
            def _():
                compute(tick, kind)
                if kind == 0:
                    @pl.when(turn == 0)
                    def _():
                        pl.semaphore_wait(barrier, len(partners))
                core_copy(tick).start()

            for lag, stage in zip(LAGS, stages):
                group = tick - lag

                @pl.when(jnp.logical_and(group >= 0, group < GROUPS))
                def _(group=group, stage=stage):
                    stage(group, 1 - kind)
        return carry

    lax.fori_loop(0, (GROUPS + LAGS[-1] + 1) // 2, two_ticks, 0)

    def drain(half, carry):
        for kind in range(2):
            group = 2 * half + kind
            core_copy(group).wait_send()
            first_copy(group, kind).wait_send()
            second_copy(group, kind).wait_send()
            for n in range(3):
                z_copy(group, n).wait_send()
        return carry

    lax.fori_loop(0, GROUPS // 2, drain, 0)


def on_device(integrals, coeffs, shell_pairs, block_count):
    slots, width, columns = integrals.shape
    occ = coeffs.shape[1]
    kets = columns // width
    shells = coeffs.shape[0] // width
    tile = (16, occ)
    bf16 = jnp.bfloat16
    hbm = pl.BlockSpec(memory_space=pltpu.HBM)
    smem = pl.BlockSpec(memory_space=pltpu.SMEM)
    out = pl.pallas_call(
        transform_kernel,
        out_shape=jax.ShapeDtypeStruct((GROUPS,) + tile, jnp.float32),
        in_specs=[smem, smem, hbm, hbm],
        out_specs=pl.BlockSpec(memory_space=pltpu.VMEM),
        scratch_shapes=[
            pltpu.VMEM((shells, width, occ), bf16),
            pltpu.VMEM(integrals.shape, bf16),
            pltpu.VMEM((2, occ // 8, 8, 4 * width), jnp.float32),
            pltpu.VMEM((2, occ, 4 * width), bf16),
            pltpu.VMEM((slots * width, occ), bf16),
            pltpu.VMEM((2, 2, 2, 4 * width, 4 * width), bf16),
            pltpu.VMEM((2, 2 * occ, slots * width), bf16),
            pltpu.VMEM((GROUPS, 4, 2, 2) + tile, jnp.float32),
            pltpu.VMEM((GROUPS, 4, 2, 2) + tile, bf16),
            pltpu.VMEM((GROUPS, 4, 2, 2) + tile, bf16),
            pltpu.VMEM((GROUPS, 4, 2) + tile, bf16),
            pltpu.VMEM((GROUPS, 4, 2) + tile, bf16),
            pltpu.VMEM((GROUPS, 4) + tile, bf16),
            pltpu.VMEM((GROUPS, 4) + tile, bf16),
            pltpu.VMEM((GROUPS, 3) + tile, bf16),
            pltpu.VMEM((GROUPS, 3) + tile, bf16),
            pltpu.SemaphoreType.DMA((2,)),
            pltpu.SemaphoreType.DMA((GROUPS, 6)),
            pltpu.SemaphoreType.DMA((GROUPS, 6)),
        ],
        compiler_params=pltpu.CompilerParams(
            collective_id=0, has_side_effects=True, vmem_limit_bytes=53 * 1024 * 1024
        ),
    )(shell_pairs.T, block_count, coeffs.reshape(shells, width, occ), integrals)
    return out.reshape(kets, occ // 32, occ).transpose(1, 0, 2)


def on_device_general(integrals, coeffs, shell_pairs, block_count):
    slot_count = integrals.shape[0]
    shell_size = integrals.shape[1]
    ket_count = integrals.shape[2] // shell_size
    occ_count = coeffs.shape[1]
    shell_count = coeffs.shape[0] // shell_size
    pair_count = lax.axis_size("pair")
    red_count = lax.axis_size("red")
    pair_index = lax.axis_index("pair")
    red_index = lax.axis_index("red")
    owned_rows = occ_count // pair_count
    coef_table = coeffs.reshape(shell_count, shell_size, occ_count)
    first_slot = (pair_index * red_count + red_index) * slot_count
    own_pairs = lax.dynamic_slice_in_dim(shell_pairs, first_slot, slot_count, 0)
    live_mask = (jnp.arange(slot_count, dtype=jnp.int32) < block_count[0, 0]).astype(jnp.float32)
    left_panels = jnp.take(coef_table, own_pairs[:, 0], axis=0)
    half_done = jnp.einsum(
        "kmi,kmx->kix", left_panels, integrals, preferred_element_type=jnp.float32
    )
    half_done = (half_done * live_mask[:, None, None]).astype(jnp.bfloat16)
    right_panels = jnp.take(coef_table, own_pairs[:, 1], axis=0)
    whole_sum = jnp.einsum(
        "kpiqn,knrj->priqj",
        half_done.reshape(slot_count, pair_count, owned_rows, ket_count, shell_size),
        right_panels.reshape(slot_count, shell_size, red_count, occ_count // red_count),
        preferred_element_type=jnp.float32,
    )
    whole_sum = whole_sum.reshape(
        pair_count * red_count * owned_rows, ket_count, occ_count // red_count
    )
    return lax.psum_scatter(whole_sum, ("pair", "red"), scatter_dimension=0, tiled=True)


def solution(mesh):
    small = mesh.shape["pair"] == 32 and mesh.shape["red"] == 1
    return jax.shard_map(
        on_device if small else on_device_general,
        mesh=mesh,
        in_specs=(P(("pair", "red"), None, None), P(), P(), P("pair", "red")),
        out_specs=P("pair", None, "red"),
        check_vma=False,
    )
```

```python
import jax
import jax.numpy as jnp
from jax import lax
from jax.experimental import pallas as pl
from jax.experimental.pallas import tpu as pltpu
from jax.sharding import PartitionSpec as P

GROUPS = 12
LAGS = (1, 5, 9, 13)


def transform_kernel(
    pairs_ref, count_ref, coeffs_hbm, ints_hbm, out_ref,
    coeffs, ints, turned, left, right, diag, half,
    own, snd0, rcv0, snd1, rcv1, snd2, rcv2, snd3, rcv3,
    load_sem, send_sem, recv_sem,
):
    load_coeffs = pltpu.make_async_copy(coeffs_hbm, coeffs, load_sem.at[0])
    load_ints = pltpu.make_async_copy(ints_hbm, ints, load_sem.at[1])
    load_coeffs.start()
    load_ints.start()

    me = lax.axis_index("pair")

    def other(bit):
        return me + bit * (1 - 2 * ((me // bit) % 2))

    core_at, x_at, y_at = other(1), other(2), other(4)
    z_low, z_high = other(8) - me, other(16) - me
    z_at = (me + z_low, me + z_high, me + z_low + z_high)
    partners = (core_at, x_at, y_at) + z_at

    barrier = pltpu.get_barrier_semaphore()
    for at in partners:
        pl.semaphore_signal(
            barrier, inc=1, device_id={"pair": at}, device_id_type=pl.DeviceIdType.MESH
        )

    slots, width, columns = ints.shape
    occ = coeffs.shape[2]
    span = 4 * width
    diag[...] = jnp.zeros_like(diag)
    load_coeffs.wait()
    for k in range(slots):
        row_shell = pairs_ref[0, me * slots + k]
        col_shell = pairs_ref[1, me * slots + k]
        live = jnp.where(k < count_ref[0, 0], 1.0, 0.0).astype(jnp.float32)
        panel = coeffs[row_shell].astype(jnp.float32) * live
        turned[k // 4, :, :, pl.ds((k % 4) * width, width)] = panel.T.reshape(
            occ // 8, 8, width
        )
        right[pl.ds(k * width, width), :] = coeffs[col_shell]

    moves = [other(w) - me for w in (1, 2, 4, 8, 16)]

    def place(rel):
        at = me
        for n, move in enumerate(moves):
            if (rel >> n) % 2:
                at = at + move
        return at

    for core in range(2):
        for two in range(8):
            first = place(core + 2 * (2 * two))
            second = place(core + 2 * (2 * two + 1))
            for part in range(2):
                rows = jnp.concatenate([turned[part, first], turned[part, second]], axis=0)
                left[part, pl.ds(core * 128 + two * 16, 16), :] = rows.astype(jnp.bfloat16)

    load_ints.wait()

    lane = lax.broadcasted_iota(jnp.int32, (width, 2 * width), 1)
    low = lane < width

    def lay_out(group, kind):
        cols = pl.ds(pl.multiple_of(group * 2 * width, 2 * width), 2 * width)
        for k in range(slots):
            tile = ints[k, :, cols].astype(jnp.float32)
            swap = pltpu.roll(tile, width, 1)
            at_lane = pl.ds((k % 4) // 2 * 2 * width, 2 * width)
            at_row = pl.ds((k % 4) * width, width)
            for odd in range(2):
                source = tile if k % 2 == odd else swap
                keep = low if k % 2 == 0 else jnp.logical_not(low)
                diag[kind, odd, k // 4, at_row, at_lane] = jnp.where(keep, source, 0.0).astype(jnp.bfloat16)

    def first_half(kind):
        for odd in range(2):
            for part in range(2):
                product = jnp.dot(left[part], diag[kind, odd, part], preferred_element_type=jnp.float32)
                half[kind, pl.ds(odd * occ, occ), pl.ds(part * span, span)] = product.astype(jnp.bfloat16)

    def second_half(group, kind):
        done = jnp.dot(half[kind], right[...], preferred_element_type=jnp.float32)
        done = done.reshape(2, 2, 4, 2, 2, 8, occ)
        both = jnp.concatenate([done[0], done[1]], axis=4)
        own[group] = both[0]
        snd0[group] = both[1].astype(jnp.bfloat16)

    def compute(group, kind):
        second_half(group, kind)
        first_half(1 - kind)
        lay_out((group + 2) % GROUPS, kind)

    lay_out(0, 0)
    first_half(0)
    lay_out(1, 1)

    def copy(group, stage, source, target, at):
        return pltpu.make_async_remote_copy(
            src_ref=source,
            dst_ref=target,
            send_sem=send_sem.at[group, stage],
            recv_sem=recv_sem.at[group, stage],
            device_id={"pair": at},
            device_id_type=pl.DeviceIdType.MESH,
        )

    def core_copy(group):
        return copy(group, 0, snd0.at[group], rcv0.at[group], core_at)

    def first_copy(group, kind):
        at = y_at if kind else x_at
        return copy(group, 1, snd1.at[group], rcv1.at[group], at)

    def second_copy(group, kind):
        at = x_at if kind else y_at
        return copy(group, 2, snd2.at[group], rcv2.at[group], at)

    def z_copy(group, n):
        return copy(group, 3 + n, snd3.at[group, n], rcv3.at[group, n], z_at[n])

    def chunks(group, kind, z, a, b):
        y, x = (a, b) if kind == 0 else (b, a)
        return own[group, z, y, x] + rcv0[group, z, y, x].astype(jnp.float32)

    def stage1(group, kind):
        core_copy(group).wait_recv()
        snd1[group] = chunks(group, kind, slice(None), slice(None), 1).astype(jnp.bfloat16)
        first_copy(group, kind).start()

    def stage2(group, kind):
        first_copy(group, kind).wait_recv()
        total = chunks(group, kind, slice(None), 1, 0) + rcv1[group, :, 1].astype(jnp.float32)
        snd2[group] = total.astype(jnp.bfloat16)
        second_copy(group, kind).start()

    def gathered(group, kind, z):
        return (
            chunks(group, kind, z, 0, 0)
            + rcv1[group, z, 0].astype(jnp.float32)
            + rcv2[group, z].astype(jnp.float32)
        )

    def stage3(group, kind):
        second_copy(group, kind).wait_recv()
        for n in (1, 2, 0):
            snd3[group, n] = gathered(group, kind, n + 1).astype(jnp.bfloat16)
            z_copy(group, n).start()

    def finish(group, kind):
        total = gathered(group, kind, 0)
        for n in range(3):
            z_copy(group, n).wait_recv()
        total = total + jnp.sum(rcv3[group].astype(jnp.float32), axis=0)
        out_ref[group] = total

    stages = (stage1, stage2, stage3, finish)

    def two_ticks(turn, carry):
        for kind in range(2):
            tick = 2 * turn + kind

            @pl.when(tick < GROUPS)
            def _():
                compute(tick, kind)
                if kind == 0:
                    @pl.when(turn == 0)
                    def _():
                        pl.semaphore_wait(barrier, len(partners))
                core_copy(tick).start()

            for lag, stage in zip(LAGS, stages):
                group = tick - lag

                @pl.when(jnp.logical_and(group >= 0, group < GROUPS))
                def _(group=group, stage=stage):
                    stage(group, 1 - kind)
        return carry

    lax.fori_loop(0, (GROUPS + LAGS[-1] + 1) // 2, two_ticks, 0)

    def drain(half, carry):
        for kind in range(2):
            group = 2 * half + kind
            core_copy(group).wait_send()
            first_copy(group, kind).wait_send()
            second_copy(group, kind).wait_send()
            for n in range(3):
                z_copy(group, n).wait_send()
        return carry

    lax.fori_loop(0, GROUPS // 2, drain, 0)


def on_device(integrals, coeffs, shell_pairs, block_count):
    slots, width, columns = integrals.shape
    occ = coeffs.shape[1]
    kets = columns // width
    shells = coeffs.shape[0] // width
    tile = (16, occ)
    bf16 = jnp.bfloat16
    hbm = pl.BlockSpec(memory_space=pltpu.HBM)
    smem = pl.BlockSpec(memory_space=pltpu.SMEM)
    out = pl.pallas_call(
        transform_kernel,
        out_shape=jax.ShapeDtypeStruct((GROUPS,) + tile, jnp.float32),
        in_specs=[smem, smem, hbm, hbm],
        out_specs=pl.BlockSpec(memory_space=pltpu.VMEM),
        scratch_shapes=[
            pltpu.VMEM((shells, width, occ), bf16),
            pltpu.VMEM(integrals.shape, bf16),
            pltpu.VMEM((2, occ // 8, 8, 4 * width), jnp.float32),
            pltpu.VMEM((2, occ, 4 * width), bf16),
            pltpu.VMEM((slots * width, occ), bf16),
            pltpu.VMEM((2, 2, 2, 4 * width, 4 * width), bf16),
            pltpu.VMEM((2, 2 * occ, slots * width), bf16),
            pltpu.VMEM((GROUPS, 4, 2, 2) + tile, jnp.float32),
            pltpu.VMEM((GROUPS, 4, 2, 2) + tile, bf16),
            pltpu.VMEM((GROUPS, 4, 2, 2) + tile, bf16),
            pltpu.VMEM((GROUPS, 4, 2) + tile, bf16),
            pltpu.VMEM((GROUPS, 4, 2) + tile, bf16),
            pltpu.VMEM((GROUPS, 4) + tile, bf16),
            pltpu.VMEM((GROUPS, 4) + tile, bf16),
            pltpu.VMEM((GROUPS, 3) + tile, bf16),
            pltpu.VMEM((GROUPS, 3) + tile, bf16),
            pltpu.SemaphoreType.DMA((2,)),
            pltpu.SemaphoreType.DMA((GROUPS, 6)),
            pltpu.SemaphoreType.DMA((GROUPS, 6)),
        ],
        compiler_params=pltpu.CompilerParams(
            collective_id=0, has_side_effects=True, vmem_limit_bytes=53 * 1024 * 1024
        ),
    )(shell_pairs.T, block_count, coeffs.reshape(shells, width, occ), integrals)
    return out.reshape(kets, occ // 32, occ).transpose(1, 0, 2)


def on_device_general(integrals, coeffs, shell_pairs, block_count):
    slot_count = integrals.shape[0]
    shell_size = integrals.shape[1]
    ket_count = integrals.shape[2] // shell_size
    occ_count = coeffs.shape[1]
    shell_count = coeffs.shape[0] // shell_size
    pair_count = lax.axis_size("pair")
    red_count = lax.axis_size("red")
    pair_index = lax.axis_index("pair")
    red_index = lax.axis_index("red")
    owned_rows = occ_count // pair_count
    coef_table = coeffs.reshape(shell_count, shell_size, occ_count)
    first_slot = (pair_index * red_count + red_index) * slot_count
    own_pairs = lax.dynamic_slice_in_dim(shell_pairs, first_slot, slot_count, 0)
    live_mask = (jnp.arange(slot_count, dtype=jnp.int32) < block_count[0, 0]).astype(jnp.float32)
    left_panels = jnp.take(coef_table, own_pairs[:, 0], axis=0)
    half_done = jnp.einsum(
        "kmi,kmx->kix", left_panels, integrals, preferred_element_type=jnp.float32
    )
    half_done = (half_done * live_mask[:, None, None]).astype(jnp.bfloat16)
    right_panels = jnp.take(coef_table, own_pairs[:, 1], axis=0)
    whole_sum = jnp.einsum(
        "kpiqn,knrj->priqj",
        half_done.reshape(slot_count, pair_count, owned_rows, ket_count, shell_size),
        right_panels.reshape(slot_count, shell_size, red_count, occ_count // red_count),
        preferred_element_type=jnp.float32,
    )
    whole_sum = whole_sum.reshape(
        pair_count * red_count * owned_rows, ket_count, occ_count // red_count
    )
    return lax.psum_scatter(whole_sum, ("pair", "red"), scatter_dimension=0, tiled=True)


def solution(mesh):
    small = mesh.shape["pair"] == 32 and mesh.shape["red"] == 1
    return jax.shard_map(
        on_device if small else on_device_general,
        mesh=mesh,
        in_specs=(P(("pair", "red"), None, None), P(), P(), P("pair", "red")),
        out_specs=P("pair", None, "red"),
        check_vma=False,
    )
```

```python
import jax
import jax.numpy as jnp
from jax import lax
from jax.experimental import pallas as pl
from jax.experimental.pallas import tpu as pltpu
from jax.sharding import PartitionSpec as P

GROUPS = 12
LAGS = (1, 5, 9, 13)


def transform_kernel(
    pairs_ref, count_ref, coeffs_hbm, ints_hbm, out_ref,
    coeffs, ints, turned, left, right, diag,
    own, snd0, rcv0, snd1, rcv1, snd2, rcv2, snd3, rcv3,
    load_sem, send_sem, recv_sem,
):
    load_coeffs = pltpu.make_async_copy(coeffs_hbm, coeffs, load_sem.at[0])
    load_ints = pltpu.make_async_copy(ints_hbm, ints, load_sem.at[1])
    load_coeffs.start()
    load_ints.start()

    me = lax.axis_index("pair")

    def other(bit):
        return me + bit * (1 - 2 * ((me // bit) % 2))

    core_at, x_at, y_at = other(1), other(2), other(4)
    z_low, z_high = other(8) - me, other(16) - me
    z_at = (me + z_low, me + z_high, me + z_low + z_high)
    partners = (core_at, x_at, y_at) + z_at

    barrier = pltpu.get_barrier_semaphore()
    for at in partners:
        pl.semaphore_signal(
            barrier, inc=1, device_id={"pair": at}, device_id_type=pl.DeviceIdType.MESH
        )

    slots, width, columns = ints.shape
    occ = coeffs.shape[2]
    span = 4 * width
    diag[...] = jnp.zeros_like(diag)
    load_coeffs.wait()
    for k in range(slots):
        row_shell = pairs_ref[0, me * slots + k]
        col_shell = pairs_ref[1, me * slots + k]
        live = jnp.where(k < count_ref[0, 0], 1.0, 0.0).astype(jnp.float32)
        panel = coeffs[row_shell].astype(jnp.float32) * live
        turned[k // 4, :, :, pl.ds((k % 4) * width, width)] = panel.T.reshape(
            occ // 8, 8, width
        )
        right[pl.ds(k * width, width), :] = coeffs[col_shell]

    moves = [other(w) - me for w in (1, 2, 4, 8, 16)]

    def place(rel):
        at = me
        for n, move in enumerate(moves):
            if (rel >> n) % 2:
                at = at + move
        return at

    for core in range(2):
        for two in range(8):
            first = place(core + 2 * (2 * two))
            second = place(core + 2 * (2 * two + 1))
            for part in range(2):
                rows = jnp.concatenate([turned[part, first], turned[part, second]], axis=0)
                left[part, pl.ds(core * 128 + two * 16, 16), :] = rows.astype(jnp.bfloat16)

    load_ints.wait()

    lane = lax.broadcasted_iota(jnp.int32, (width, 2 * width), 1)
    low = lane < width
    per_group = columns // (2 * width) // GROUPS

    def compute(group):
        def one_pair(step, carry):
            cols = pl.ds(pl.multiple_of((group * per_group + step) * 2 * width, 2 * width), 2 * width)
            for k in range(slots):
                tile = ints[k, :, cols].astype(jnp.float32)
                swap = pltpu.roll(tile, width, 1)
                at_lane = pl.ds((k % 4) // 2 * 2 * width, 2 * width)
                at_row = pl.ds((k % 4) * width, width)
                for odd in range(2):
                    source = tile if k % 2 == odd else swap
                    keep = low if k % 2 == 0 else jnp.logical_not(low)
                    diag[odd, k // 4, at_row, at_lane] = jnp.where(keep, source, 0.0).astype(jnp.bfloat16)
            half = jnp.concatenate(
                [
                    jnp.concatenate(
                        [
                            jnp.dot(left[part], diag[odd, part], preferred_element_type=jnp.float32).astype(jnp.bfloat16)
                            for part in range(2)
                        ],
                        axis=1,
                    )
                    for odd in range(2)
                ],
                axis=0,
            )
            done = jnp.dot(half, right[...], preferred_element_type=jnp.float32)
            done = done.reshape(2, 2, 4, 2, 2, 8, occ)
            both = jnp.concatenate([done[0], done[1]], axis=4)
            own[group, :, :, :, step] = both[0]
            snd0[group, :, :, :, step] = both[1].astype(jnp.bfloat16)
            return carry

        lax.fori_loop(0, per_group, one_pair, 0)

    def copy(group, stage, source, target, at):
        return pltpu.make_async_remote_copy(
            src_ref=source,
            dst_ref=target,
            send_sem=send_sem.at[group, stage],
            recv_sem=recv_sem.at[group, stage],
            device_id={"pair": at},
            device_id_type=pl.DeviceIdType.MESH,
        )

    def core_copy(group):
        return copy(group, 0, snd0.at[group], rcv0.at[group], core_at)

    def first_copy(group, kind):
        at = y_at if kind else x_at
        return copy(group, 1, snd1.at[group], rcv1.at[group], at)

    def second_copy(group, kind):
        at = x_at if kind else y_at
        return copy(group, 2, snd2.at[group], rcv2.at[group], at)

    def z_copy(group, n):
        return copy(group, 3 + n, snd3.at[group, n], rcv3.at[group, n], z_at[n])

    def chunks(group, kind, z, a, b):
        y, x = (a, b) if kind == 0 else (b, a)
        return own[group, z, y, x] + rcv0[group, z, y, x].astype(jnp.float32)

    def stage1(group, kind):
        core_copy(group).wait_recv()
        snd1[group] = chunks(group, kind, slice(None), slice(None), 1).astype(jnp.bfloat16)
        first_copy(group, kind).start()

    def stage2(group, kind):
        first_copy(group, kind).wait_recv()
        total = chunks(group, kind, slice(None), 1, 0) + rcv1[group, :, 1].astype(jnp.float32)
        snd2[group] = total.astype(jnp.bfloat16)
        second_copy(group, kind).start()

    def gathered(group, kind, z):
        return (
            chunks(group, kind, z, 0, 0)
            + rcv1[group, z, 0].astype(jnp.float32)
            + rcv2[group, z].astype(jnp.float32)
        )

    def stage3(group, kind):
        second_copy(group, kind).wait_recv()
        for n in (1, 2, 0):
            snd3[group, n] = gathered(group, kind, n + 1).astype(jnp.bfloat16)
            z_copy(group, n).start()

    def finish(group, kind):
        total = gathered(group, kind, 0)
        for n in range(3):
            z_copy(group, n).wait_recv()
        total = total + jnp.sum(rcv3[group].astype(jnp.float32), axis=0)
        out_ref[group] = total

    plan = tuple(zip(LAGS, (stage1, stage2, stage3, finish)))
    plan = plan[1:] + plan[:1]

    def two_ticks(turn, carry):
        for kind in range(2):
            tick = 2 * turn + kind

            @pl.when(tick < GROUPS)
            def _():
                compute(tick)
                if kind == 0:
                    @pl.when(turn == 0)
                    def _():
                        pl.semaphore_wait(barrier, len(partners))
                core_copy(tick).start()

            for lag, stage in plan:
                group = tick - lag

                @pl.when(jnp.logical_and(group >= 0, group < GROUPS))
                def _(group=group, stage=stage):
                    stage(group, 1 - kind)
        return carry

    lax.fori_loop(0, (GROUPS + LAGS[-1] + 1) // 2, two_ticks, 0)

    def drain(half, carry):
        for kind in range(2):
            group = 2 * half + kind
            core_copy(group).wait_send()
            first_copy(group, kind).wait_send()
            second_copy(group, kind).wait_send()
            for n in range(3):
                z_copy(group, n).wait_send()
        return carry

    lax.fori_loop(0, GROUPS // 2, drain, 0)


def on_device(integrals, coeffs, shell_pairs, block_count):
    slots, width, columns = integrals.shape
    occ = coeffs.shape[1]
    kets = columns // width
    shells = coeffs.shape[0] // width
    per_group = kets // 2 // GROUPS
    tile = (per_group, 16, occ)
    bf16 = jnp.bfloat16
    hbm = pl.BlockSpec(memory_space=pltpu.HBM)
    smem = pl.BlockSpec(memory_space=pltpu.SMEM)
    out = pl.pallas_call(
        transform_kernel,
        out_shape=jax.ShapeDtypeStruct((GROUPS,) + tile, jnp.float32),
        in_specs=[smem, smem, hbm, hbm],
        out_specs=pl.BlockSpec(memory_space=pltpu.VMEM),
        scratch_shapes=[
            pltpu.VMEM((shells, width, occ), bf16),
            pltpu.VMEM(integrals.shape, bf16),
            pltpu.VMEM((2, occ // 8, 8, 4 * width), jnp.float32),
            pltpu.VMEM((2, occ, 4 * width), bf16),
            pltpu.VMEM((slots * width, occ), bf16),
            pltpu.VMEM((2, 2, 4 * width, 4 * width), bf16),
            pltpu.VMEM((GROUPS, 4, 2, 2) + tile, jnp.float32),
            pltpu.VMEM((GROUPS, 4, 2, 2) + tile, bf16),
            pltpu.VMEM((GROUPS, 4, 2, 2) + tile, bf16),
            pltpu.VMEM((GROUPS, 4, 2) + tile, bf16),
            pltpu.VMEM((GROUPS, 4, 2) + tile, bf16),
            pltpu.VMEM((GROUPS, 4) + tile, bf16),
            pltpu.VMEM((GROUPS, 4) + tile, bf16),
            pltpu.VMEM((GROUPS, 3) + tile, bf16),
            pltpu.VMEM((GROUPS, 3) + tile, bf16),
            pltpu.SemaphoreType.DMA((2,)),
            pltpu.SemaphoreType.DMA((GROUPS, 6)),
            pltpu.SemaphoreType.DMA((GROUPS, 6)),
        ],
        compiler_params=pltpu.CompilerParams(
            collective_id=0, has_side_effects=True, vmem_limit_bytes=53 * 1024 * 1024
        ),
    )(shell_pairs.T, block_count, coeffs.reshape(shells, width, occ), integrals)
    return out.reshape(kets, occ // 32, occ).transpose(1, 0, 2)


def on_device_general(integrals, coeffs, shell_pairs, block_count):
    slot_count = integrals.shape[0]
    shell_size = integrals.shape[1]
    ket_count = integrals.shape[2] // shell_size
    occ_count = coeffs.shape[1]
    shell_count = coeffs.shape[0] // shell_size
    pair_count = lax.axis_size("pair")
    red_count = lax.axis_size("red")
    pair_index = lax.axis_index("pair")
    red_index = lax.axis_index("red")
    owned_rows = occ_count // pair_count
    coef_table = coeffs.reshape(shell_count, shell_size, occ_count)
    first_slot = (pair_index * red_count + red_index) * slot_count
    own_pairs = lax.dynamic_slice_in_dim(shell_pairs, first_slot, slot_count, 0)
    live_mask = (jnp.arange(slot_count, dtype=jnp.int32) < block_count[0, 0]).astype(jnp.float32)
    left_panels = jnp.take(coef_table, own_pairs[:, 0], axis=0)
    half_done = jnp.einsum(
        "kmi,kmx->kix", left_panels, integrals, preferred_element_type=jnp.float32
    )
    half_done = (half_done * live_mask[:, None, None]).astype(jnp.bfloat16)
    right_panels = jnp.take(coef_table, own_pairs[:, 1], axis=0)
    whole_sum = jnp.einsum(
        "kpiqn,knrj->priqj",
        half_done.reshape(slot_count, pair_count, owned_rows, ket_count, shell_size),
        right_panels.reshape(slot_count, shell_size, red_count, occ_count // red_count),
        preferred_element_type=jnp.float32,
    )
    whole_sum = whole_sum.reshape(
        pair_count * red_count * owned_rows, ket_count, occ_count // red_count
    )
    return lax.psum_scatter(whole_sum, ("pair", "red"), scatter_dimension=0, tiled=True)


def solution(mesh):
    small = mesh.shape["pair"] == 32 and mesh.shape["red"] == 1
    return jax.shard_map(
        on_device if small else on_device_general,
        mesh=mesh,
        in_specs=(P(("pair", "red"), None, None), P(), P(), P("pair", "red")),
        out_specs=P("pair", None, "red"),
        check_vma=False,
    )
```
